512 devices in a mesh: seq: 32 (over z, y_lo), mp: 16 (over x, y_hi, core).
Axes of the slice: x: 4, y: 4 (y_hi: 2, y_lo: 2; y = y_hi * 2 + y_lo), z: 16, core: 2. Of those that a mesh axis runs over, the one named last changes fastest.
Arguments:
- queries: bfloat16 [16384, 8192], P('seq', 'mp'), may hold values from -6 to 6
- keys_in: bfloat16 [16384, 8192], P('seq', 'mp'), may hold values from -6 to 6
- values_in: bfloat16 [16384, 8192], P('seq', 'mp'), may hold values from -6 to 6
- residual: bfloat16 [16384, 8192], P('seq', 'mp')
- short_taps: bfloat16 [3, 7, 8192], P(None, None, 'mp'), may hold values from -2 to 2
- mr_filter: bfloat16 [128, 512], P('seq', 'mp'), may hold values from -0.5 to 0.5
- norm_gain: bfloat16 [8192], P('mp'), may hold values from 0.5 to 1.5
- predecessor: int32 [32], replicated, may hold values from -1 to 31, as said below
- stretch_lengths: int32 [32], replicated, may hold values from 1 to 512, as said below
Outputs:
- mixed: bfloat16 [16384, 8192], P('seq', 'mp')
- normed: bfloat16 [16384, 8192], P('seq', 'mp')
The draws below stay inside these ranges and needn't reach their ends.
Inputs may be any that keep to these rules, and one draw needn't show every extreme that they name: predecessor[j] is the stretch holding the preceding 512 tokens of stretch j's genome, or -1 for a genome's first stretch; each stretch precedes at most one stretch, and the chains have no cycles. `stretch_lengths`: every stretch that precedes another stretch is full (512 valid tokens); valid tokens come first.
All inputs are finite; a program needn't handle non-finite values.
Results may differ from the reference program's by a relative error of at most 0.0049.
Values may be sent and summed in bfloat16 or wider, within the bound.
A program may use at most 64 MiB of HBM per device.

```python
import jax
import jax.numpy as jnp
from jax import lax

D = 8192
GSIZE = 16
GROUPS = 512
TAPS = 128
SHORT = 7
TOK_DEV = 512
STRETCHES = 32
TOKENS = 16384


def draw_residual(key, part):
    first, second = jax.random.split(jax.random.fold_in(key, 11), 2)
    column_scale = 10.0 ** (jnp.arange(D, dtype=jnp.float32) / D)
    row_scale = 10.0 ** jax.random.uniform(second, (TOKENS, 1), jnp.float32)
    base = jax.random.normal(first, (TOKENS, D), jnp.float32)
    return (0.3 * base * row_scale * column_scale[None, :]).astype(jnp.bfloat16)


def chain_layout(key):
    base = jax.random.fold_in(key, 7)
    first, second, third = jax.random.split(base, 3)
    rest = jax.random.permutation(first, STRETCHES - 1).astype(jnp.int32)
    target = STRETCHES // 2 - 1
    head_value = rest[0]
    rest = jnp.where(rest == target, head_value, rest)
    rest = rest.at[0].set(target).astype(jnp.int32)
    order = jnp.concatenate([jnp.full((1,), STRETCHES - 1, jnp.int32), rest])
    position = jnp.arange(STRETCHES, dtype=jnp.int32)
    coins = jax.random.randint(second, (STRETCHES,), 0, 4) == 0
    starts = (position == 0) | coins & (position != 1)
    before = jnp.concatenate([jnp.zeros((1,), jnp.int32), order[:-1]])
    pred_pos = jnp.where(starts, -1, before).astype(jnp.int32)
    last = jnp.concatenate([starts[1:], jnp.ones((1,), bool)])
    ragged = jax.random.randint(third, (STRETCHES,), 1, TOK_DEV + 1)
    length_pos = jnp.where(last, ragged, TOK_DEV).astype(jnp.int32)
    pred_out = jnp.zeros((STRETCHES,), jnp.int32).at[order].set(pred_pos)
    length_out = jnp.zeros((STRETCHES,), jnp.int32).at[order].set(length_pos)
    return (pred_out, length_out)


def draw_predecessor(key, part):
    return chain_layout(key)[0]


def draw_stretch_lengths(key, part):
    return chain_layout(key)[1]


def shard_levels(rng, extent, shards, low, top_value):
    level, own = 1.0, jax.random.fold_in(rng, 6)
    for dim, parts in shards:
        steps = jnp.exp(jax.random.uniform(jax.random.fold_in(own, dim), (parts,), jnp.float32, low / len(shards), top_value / len(shards)))
        level = level * jnp.repeat(steps, extent[dim] // parts).reshape([-1 if axis == dim else 1 for axis in range(len(extent))])
    return level


def noise(stream_key, shape, scale, reach, cuts=(), kind=jnp.bfloat16):
    array = jax.random.normal(stream_key, shape, jnp.float32) * scale
    if len(cuts) > 0:
        array = shard_levels(stream_key, shape, cuts, -0.22, 0.18) * array
    return jnp.clip(array, min=-reach, max=reach).astype(kind)


def setup_inputs(seed: int = 0) -> dict:
    seeds = jax.random.split(jax.random.key(seed), 10)
    queries = noise(seeds[0], (TOKENS, D), 1.0, 6.0, ((0, 32), (1, 16)))
    keys_in = noise(seeds[1], (TOKENS, D), 1.0, 6.0, ((0, 32), (1, 16)))
    values_in = noise(seeds[2], (TOKENS, D), 1.0, 6.0, ((0, 32), (1, 16)))
    residual = draw_residual(jax.random.fold_in(seeds[9], 71), 0)
    short_taps = noise(seeds[4], (3, SHORT, D), SHORT ** -0.5, 2.0, ((2, 16),))
    mr_filter = noise(seeds[5], (TAPS, GROUPS), TAPS ** -0.5, 0.5, ((0, 32), (1, 16)))
    norm_gain = jnp.clip(1.0 + 0.1 * jax.random.normal(seeds[6], (D,), jnp.float32), 0.5, 1.5).astype(jnp.bfloat16)
    predecessor = draw_predecessor(jax.random.fold_in(seeds[9], 71), 0)
    stretch_lengths = draw_stretch_lengths(jax.random.fold_in(seeds[9], 71), 0)
    return dict(queries=queries, keys_in=keys_in, values_in=values_in, residual=residual, short_taps=short_taps, mr_filter=mr_filter, norm_gain=norm_gain, predecessor=predecessor, stretch_lengths=stretch_lengths)


EPSILON = 1e-06

def featurize(extended, taps):
    length = extended.shape[0] - 8
    total = jnp.zeros((length, extended.shape[1]), jnp.float32)
    for offset in range(taps.shape[0]):
        total = total + taps[offset].astype(jnp.float32) * extended[8 - offset:8 - offset + length].astype(jnp.float32)
    return total

def toeplitz_blocks(filter_rows):
    tap_count = filter_rows.shape[0]
    group_count = filter_rows.shape[1]
    flipped = filter_rows[::-1].T
    pattern = jnp.concatenate([jnp.zeros((group_count, 1), filter_rows.dtype), flipped, jnp.zeros((group_count, tap_count), filter_rows.dtype)], axis=1)
    tiled = jnp.tile(pattern, (1, tap_count))[:, :2 * tap_count * tap_count]
    return tiled.reshape(group_count, tap_count, 2 * tap_count)

def long_conv(extended, filter_rows, group_size):
    tap_count = filter_rows.shape[0]
    length = extended.shape[0] - tap_count
    blocks = length // tap_count
    channels = extended.shape[1]
    pieces = extended.reshape(blocks + 1, tap_count, channels)
    windows = jnp.concatenate([pieces[:-1], pieces[1:]], axis=1).reshape(blocks, 2 * tap_count, channels // group_size, group_size)
    matrices = toeplitz_blocks(filter_rows)
    result = jnp.einsum('gij,bjgc->bigc', matrices.astype(jnp.float32), windows.astype(jnp.float32))
    return result.reshape(length, channels)

def tail_of(stretched, source, count):
    present = source >= 0
    clipped = jnp.clip(source, 0, STRETCHES - 1).astype(jnp.int32)
    whole = lax.dynamic_index_in_dim(stretched, clipped, 0, keepdims=False)
    tail = whole[whole.shape[0] - count:]
    return jnp.where(present, tail, jnp.zeros_like(tail))

def reference(queries, keys_in, values_in, residual, short_taps, mr_filter, norm_gain, predecessor, stretch_lengths):
    stretch_query = queries.reshape(STRETCHES, TOK_DEV, D)
    stretch_key = keys_in.reshape(STRETCHES, TOK_DEV, D)
    stretch_value = values_in.reshape(STRETCHES, TOK_DEV, D)
    stretch_resid = residual.reshape(STRETCHES, TOK_DEV, D)

    def first_pass(index):
        source = predecessor[index]
        key_ext = jnp.concatenate([tail_of(stretch_key, source, 8), lax.dynamic_index_in_dim(stretch_key, index, 0, keepdims=False)])
        value_ext = jnp.concatenate([tail_of(stretch_value, source, 8), lax.dynamic_index_in_dim(stretch_value, index, 0, keepdims=False)])
        return (featurize(key_ext, short_taps[1]) * featurize(value_ext, short_taps[2])).astype(jnp.bfloat16)
    indices = jnp.arange(STRETCHES, dtype=jnp.int32)
    mixed_all = lax.map(first_pass, indices)

    def second_pass(index):
        source = predecessor[index]
        query_ext = jnp.concatenate([tail_of(stretch_query, source, 8), lax.dynamic_index_in_dim(stretch_query, index, 0, keepdims=False)])
        query_feat = featurize(query_ext, short_taps[0])
        extended = jnp.concatenate([tail_of(mixed_all, source, TAPS), lax.dynamic_index_in_dim(mixed_all, index, 0, keepdims=False)])
        filtered = long_conv(extended, mr_filter, GSIZE)
        valid = (jnp.arange(TOK_DEV, dtype=jnp.int32) < stretch_lengths[index])[:, None]
        mixed = jnp.where(valid, query_feat * filtered, 0.0).astype(jnp.bfloat16)
        summed = lax.dynamic_index_in_dim(stretch_resid, index, 0, keepdims=False).astype(jnp.float32) + mixed.astype(jnp.float32)
        total = lax.optimization_barrier(jnp.sum(summed * summed, axis=1))
        scale_rows = lax.rsqrt(total / D + EPSILON)
        normed = jnp.where(valid, summed * scale_rows[:, None] * norm_gain.astype(jnp.float32), 0.0).astype(jnp.bfloat16)
        return (mixed, normed)
    mixed_out, normed_out = lax.map(second_pass, indices)
    return (mixed_out.reshape(TOKENS, D), normed_out.reshape(TOKENS, D))
```

```python
import functools

import jax
import jax.numpy as jnp
from jax import lax
from jax.experimental import pallas as pl
from jax.experimental.pallas import tpu as pltpu
from jax.sharding import PartitionSpec as P

MESH = pl.DeviceIdType.MESH
EPSILON = 1e-06
ROWS = 512
WIDTH = 512
LANES = 128
TAPS = 128
SHORT = 7
GSIZE = 16
PAD = 16
CHUNK = 64
SLOT = 20
F32 = jnp.float32
BF16 = jnp.bfloat16


def kernel(
    n_seq,
    n_mp,
    q_hbm,
    k_hbm,
    v_hbm,
    r_hbm,
    taps_hbm,
    filt_hbm,
    gain_hbm,
    pred_ref,
    len_ref,
    mixed_hbm,
    normed_hbm,
    qbuf,
    kbuf,
    vbuf,
    rbuf,
    tapsb,
    filtb,
    gainb,
    taps,
    qfeat,
    mix,
    msg,
    recv,
    fwd,
    fin,
    rows_f,
    toep,
    flipped,
    summed,
    squares,
    mixed_v,
    normed_v,
    part,
    parts,
    load_sem,
    store_sem,
    send1,
    recv1,
    send2,
    recv2,
    send3,
    recv3,
):
    me = lax.axis_index("seq")
    mine = lax.axis_index("mp")

    barrier = pltpu.get_barrier_semaphore()

    def hello_seq(d, _):
        pl.semaphore_signal(
            barrier, inc=1, device_id={"seq": lax.rem(me + d, n_seq)}, device_id_type=MESH
        )
        return 0

    def hello_mp(d, _):
        pl.semaphore_signal(
            barrier, inc=1, device_id={"mp": lax.rem(mine + d, n_mp)}, device_id_type=MESH
        )
        return 0

    lax.fori_loop(1, n_seq, hello_seq, 0)
    lax.fori_loop(1, n_mp, hello_mp, 0)

    body = pl.ds(PAD, ROWS)
    loads = [
        pltpu.make_async_copy(k_hbm, kbuf.at[body], load_sem.at[0]),
        pltpu.make_async_copy(v_hbm, vbuf.at[body], load_sem.at[1]),
        pltpu.make_async_copy(taps_hbm, tapsb, load_sem.at[2]),
        pltpu.make_async_copy(filt_hbm, filtb, load_sem.at[3]),
        pltpu.make_async_copy(q_hbm, qbuf.at[body], load_sem.at[4]),
        pltpu.make_async_copy(r_hbm, rbuf, load_sem.at[5]),
        pltpu.make_async_copy(gain_hbm, gainb, load_sem.at[6]),
    ]
    for load in loads:
        load.start()
    for ref in (qbuf, kbuf, vbuf):
        ref[0:PAD, :] = jnp.zeros((PAD, WIDTH), BF16)
    for load in loads[:4]:
        load.wait()
    for branch in range(3):
        taps[8 * branch : 8 * branch + SHORT, :] = tapsb[branch].astype(F32)

    def featurize(ref, branch, start, count, lanes):
        ext = ref[pl.ds(start, count + PAD), lanes].astype(F32)[PAD - 8 :]
        acc = taps[pl.ds(8 * branch, 1), lanes] * ext[8:]
        for s in range(1, SHORT):
            acc = acc + taps[pl.ds(8 * branch + s, 1), lanes] * pltpu.roll(ext, s, 0)[8:]
        return acc

    def product(start, count, lanes):
        key_feat = featurize(kbuf, 1, start, count, lanes)
        value_feat = featurize(vbuf, 2, start, count, lanes)
        return (key_feat * value_feat).astype(BF16)

    tiles = WIDTH // LANES
    per_tile = ROWS // CHUNK
    tail_chunks = TAPS // CHUNK

    def tail_step(c, _):
        for b in range(tiles):
            lanes = pl.ds(b * LANES, LANES)
            start = pl.multiple_of(ROWS - TAPS + c * CHUNK, CHUNK)
            value = product(start, CHUNK, lanes)
            mix[pl.ds(TAPS + start, CHUNK), lanes] = value
            for a in range(CHUNK // 16):
                msg[(c * (CHUNK // 16) + a) * tiles + b, 0:16, :] = value[16 * a : 16 * a + 16]
        return 0

    lax.fori_loop(0, tail_chunks, tail_step, 0)

    loads[4].wait()
    for i, ref in enumerate((qbuf, kbuf, vbuf)):
        tail = ref[PAD + ROWS - 16 : PAD + ROWS, :].astype(F32)[8:]
        for b in range(tiles):
            rows_f[pl.ds(4 * b + i, 8, stride=16), :] = tail[:, b * LANES : (b + 1) * LANES]
    filt = filtb[...].astype(F32)
    share, groups = filt.shape
    row = jnp.concatenate([filt[i : i + 1] for i in range(share)], axis=1)
    for b in range(tiles):
        rows_f[pl.ds(4 * b + 3, 8, stride=16), :] = jnp.broadcast_to(row, (8, LANES))

    def pack(p, _):
        msg[p, 16:20, :] = rows_f[pl.ds(pl.multiple_of(4 * p, 4), 4), :].astype(BF16)
        return 0

    lax.fori_loop(0, n_seq, pack, 0)
    recv[me] = msg[me]

    pl.semaphore_wait(barrier, n_seq + n_mp - 2)

    def scatter(d, _):
        p = lax.rem(me + d, n_seq)
        pltpu.make_async_remote_copy(
            src_ref=msg.at[p],
            dst_ref=recv.at[me],
            send_sem=send1,
            recv_sem=recv1,
            device_id={"seq": p},
            device_id_type=MESH,
        ).start()
        return 0

    lax.fori_loop(1, n_seq, scatter, 0)

    def rest_step(c, _):
        start = pl.multiple_of(c * CHUNK, CHUNK)
        for b in range(tiles):
            lanes = pl.ds(b * LANES, LANES)
            mix[pl.ds(TAPS + start, CHUNK), lanes] = product(start, CHUNK, lanes)
        return 0

    lax.fori_loop(0, per_tile - tail_chunks, rest_step, 0)

    def query_step(c, _):
        start = pl.multiple_of(c * CHUNK, CHUNK)
        for b in range(tiles):
            lanes = pl.ds(b * LANES, LANES)
            qfeat[pl.ds(start, CHUNK), lanes] = featurize(qbuf, 0, start, CHUNK, lanes)
        return 0

    lax.fori_loop(0, per_tile, query_step, 0)
    squares[...] = jnp.zeros((ROWS, LANES), F32)

    others = pl.ds(0, n_seq - 1)
    pltpu.make_async_copy(recv.at[others], recv.at[others], recv1).wait()

    def forward(i):
        source = pred_ref[i]
        keep = (source >= 0).astype(F32)
        piece = recv[jnp.maximum(source, 0)]
        return (piece.astype(F32) * keep).astype(BF16)

    def route(d, _):
        i = lax.rem(me + d, n_seq)
        fwd[i] = forward(i)
        pltpu.make_async_remote_copy(
            src_ref=fwd.at[i],
            dst_ref=fin.at[me],
            send_sem=send2,
            recv_sem=recv2,
            device_id={"seq": i},
            device_id_type=MESH,
        ).start()
        return 0

    lax.fori_loop(1, n_seq, route, 0)
    fin[me] = forward(me)

    def unpack_recv(p, _):
        rows_f[pl.ds(pl.multiple_of(4 * p, 4), 4), :] = recv[p, 16:20, :].astype(F32)
        return 0

    lax.fori_loop(0, n_seq, unpack_recv, 0)
    gathered = rows_f[pl.ds(3, n_seq, stride=4), :]
    stacked = jnp.concatenate(
        [gathered[:, i * groups : (i + 1) * groups] for i in range(share)], axis=0
    )
    at = lax.broadcasted_iota(jnp.int32, (TAPS, LANES), 0)
    tap = share * (at & (n_seq - 1)) + at // n_seq
    place = (TAPS - tap) & (TAPS - 1)
    spread = (place == lax.broadcasted_iota(jnp.int32, (TAPS, LANES), 1)).astype(BF16)
    flipped[...] = lax.dot_general(
        stacked.astype(BF16), spread, (((0,), (0,)), ((), ())), preferred_element_type=F32
    )
    below = lax.broadcasted_iota(jnp.int32, (TAPS, LANES), 1) <= lax.broadcasted_iota(
        jnp.int32, (TAPS, LANES), 0
    )

    def toeplitz(g, _):
        first = jnp.broadcast_to(flipped[pl.ds(g, 1), :], (TAPS, LANES))
        turned = pltpu.roll(first, 0, 1, stride=1, stride_axis=0)
        rows = pl.ds(pl.multiple_of(g * TAPS, TAPS), TAPS)
        toep[rows, 0:LANES] = jnp.where(below, 0.0, turned).astype(BF16)
        toep[rows, LANES : 2 * LANES] = jnp.where(below, turned, 0.0).astype(BF16)
        return 0

    lax.fori_loop(0, groups, toeplitz, 0)

    length = len_ref[me]
    loads[5].wait()
    loads[6].wait()
    in_tile = LANES // GSIZE
    lane_group = lax.broadcasted_iota(jnp.int32, (TAPS, LANES), 1) // GSIZE

    def convolve(pair):
        def step(b, _):
            lanes = pl.ds(pl.multiple_of(b * LANES, LANES), LANES)
            window = jnp.concatenate(
                [mix[blk * TAPS : (blk + 2) * TAPS, lanes] for blk in pair], axis=1
            )
            rows = pl.ds(pl.multiple_of(b * in_tile * TAPS, TAPS), in_tile * TAPS)
            product_all = jnp.dot(toep[rows, :], window, preferred_element_type=F32)
            for half, blk in enumerate(pair):
                side = slice(half * LANES, (half + 1) * LANES)
                out = product_all[0:TAPS, side]
                for g in range(1, in_tile):
                    out = jnp.where(
                        lane_group == g, product_all[g * TAPS : (g + 1) * TAPS, side], out
                    )
                span = slice(blk * TAPS, (blk + 1) * TAPS)
                valid = (
                    lax.broadcasted_iota(jnp.int32, (TAPS, LANES), 0) + blk * TAPS
                ) < length
                mixed = jnp.where(valid, qfeat[span, lanes] * out, 0.0).astype(BF16)
                mixed_v[span, lanes] = mixed
                total = rbuf[span, lanes].astype(F32) + mixed.astype(F32)
                summed[span, lanes] = total
                squares[span, :] = squares[span, :] + total * total
            return 0

        lax.fori_loop(0, tiles, step, 0)

    def store_pair(pair, sem):
        span = pl.ds(pair[0] * TAPS, len(pair) * TAPS)
        return pltpu.make_async_copy(mixed_v.at[span], mixed_hbm.at[span], sem)

    convolve((2, 3))
    stores = [store_pair((2, 3), store_sem.at[0])]
    stores[0].start()

    pltpu.make_async_copy(fin.at[others], fin.at[others], recv2).wait()

    def unpack_fin(p, _):
        rows_f[pl.ds(pl.multiple_of(4 * p, 4), 4), :] = fin[p, 16:20, :].astype(F32)
        return 0

    lax.fori_loop(0, n_seq, unpack_fin, 0)
    for a in range(TAPS // 16):
        for b in range(tiles):
            mix[16 * a : 16 * a + 16, b * LANES : (b + 1) * LANES] = fin[a * tiles + b, 0:16, :]
    for i, ref in enumerate((qbuf, kbuf, vbuf)):
        for b in range(tiles):
            head = rows_f[pl.ds(4 * b + i, 8, stride=16), :]
            ref[0:PAD, b * LANES : (b + 1) * LANES] = jnp.concatenate(
                [jnp.zeros_like(head), head], axis=0
            ).astype(BF16)
    for b in range(tiles):
        lanes = pl.ds(b * LANES, LANES)
        mix[TAPS : TAPS + 16, lanes] = product(0, 16, lanes)
        qfeat[0:16, lanes] = featurize(qbuf, 0, 0, 16, lanes)

    convolve((0, 1))
    stores.append(store_pair((0, 1), store_sem.at[1]))
    stores[1].start()

    for blk in range(ROWS // TAPS):
        span = slice(blk * TAPS, (blk + 1) * TAPS)
        part[:, span] = jnp.sum(squares[span, :].T, axis=0, keepdims=True)
    parts[mine] = part[...]

    def share_part(d, _):
        pltpu.make_async_remote_copy(
            src_ref=part,
            dst_ref=parts.at[mine],
            send_sem=send3,
            recv_sem=recv3,
            device_id={"mp": lax.rem(mine + d, n_mp)},
            device_id_type=MESH,
        ).start()
        return 0

    lax.fori_loop(1, n_mp, share_part, 0)
    if n_mp > 1:
        peers = pl.ds(0, n_mp - 1)
        pltpu.make_async_copy(parts.at[peers], parts.at[peers], recv3).wait()
    total = jnp.sum(parts[...], axis=0)
    scale = lax.rsqrt(total / (WIDTH * n_mp) + EPSILON)
    gain = gainb[...].astype(F32)
    for blk in range(ROWS // TAPS):
        span = slice(blk * TAPS, (blk + 1) * TAPS)
        column = jnp.broadcast_to(scale[:, span], (TAPS, LANES)).T
        valid = (lax.broadcasted_iota(jnp.int32, (TAPS, LANES), 0) + blk * TAPS) < length
        for b in range(tiles):
            lanes = slice(b * LANES, (b + 1) * LANES)
            normed_v[span, lanes] = jnp.where(
                valid, summed[span, lanes] * column * gain[:, lanes], 0.0
            ).astype(BF16)
        part_rows = pl.ds(blk * TAPS, TAPS)
        stores.append(
            pltpu.make_async_copy(
                normed_v.at[part_rows], normed_hbm.at[part_rows], store_sem.at[2 + blk]
            )
        )
        stores[-1].start()

    pltpu.make_async_copy(msg.at[others], msg.at[others], send1).wait()
    pltpu.make_async_copy(fwd.at[others], fwd.at[others], send2).wait()
    if n_mp > 1:
        pltpu.make_async_copy(parts.at[peers], parts.at[peers], send3).wait()
    for store in stores:
        store.wait()


def body(n_seq, n_mp, queries, keys_in, values_in, residual, short_taps, mr_filter, norm_gain, predecessor, stretch_lengths):
    whole = pl.BlockSpec(memory_space=pl.ANY)
    scalars = pl.BlockSpec(memory_space=pltpu.SMEM)
    slots = (n_seq, SLOT, LANES)
    share, groups = mr_filter.shape
    out = jax.ShapeDtypeStruct((ROWS, WIDTH), BF16)
    return pl.pallas_call(
        functools.partial(kernel, n_seq, n_mp),
        out_shape=(out, out),
        in_specs=[whole] * 7 + [scalars] * 2,
        out_specs=(whole, whole),
        scratch_shapes=[
            pltpu.VMEM((PAD + ROWS, WIDTH), BF16),
            pltpu.VMEM((PAD + ROWS, WIDTH), BF16),
            pltpu.VMEM((PAD + ROWS, WIDTH), BF16),
            pltpu.VMEM((ROWS, WIDTH), BF16),
            pltpu.VMEM((3, SHORT, WIDTH), BF16),
            pltpu.VMEM((share, groups), BF16),
            pltpu.VMEM((1, WIDTH), BF16),
            pltpu.VMEM((24, WIDTH), F32),
            pltpu.VMEM((ROWS, WIDTH), F32),
            pltpu.VMEM((TAPS + ROWS, WIDTH), BF16),
            pltpu.VMEM(slots, BF16),
            pltpu.VMEM(slots, BF16),
            pltpu.VMEM(slots, BF16),
            pltpu.VMEM(slots, BF16),
            pltpu.VMEM((LANES, LANES), F32),
            pltpu.VMEM((groups * TAPS, 2 * TAPS), BF16),
            pltpu.VMEM((groups, LANES), F32),
            pltpu.VMEM((ROWS, WIDTH), F32),
            pltpu.VMEM((ROWS, LANES), F32),
            pltpu.VMEM((ROWS, WIDTH), BF16),
            pltpu.VMEM((ROWS, WIDTH), BF16),
            pltpu.VMEM((1, ROWS), F32),
            pltpu.VMEM((n_mp, 1, ROWS), F32),
            pltpu.SemaphoreType.DMA((7,)),
            pltpu.SemaphoreType.DMA((6,)),
            pltpu.SemaphoreType.DMA,
            pltpu.SemaphoreType.DMA,
            pltpu.SemaphoreType.DMA,
            pltpu.SemaphoreType.DMA,
            pltpu.SemaphoreType.DMA,
            pltpu.SemaphoreType.DMA,
        ],
        compiler_params=pltpu.CompilerParams(
            collective_id=0, has_side_effects=True, vmem_limit_bytes=40 * 1024 * 1024
        ),
    )(
        queries,
        keys_in,
        values_in,
        residual,
        short_taps,
        mr_filter,
        norm_gain.reshape(1, WIDTH),
        predecessor,
        stretch_lengths,
    )


def solution(mesh):
    in_specs = (
        P("seq", "mp"),
        P("seq", "mp"),
        P("seq", "mp"),
        P("seq", "mp"),
        P(None, None, "mp"),
        P("seq", "mp"),
        P("mp"),
        P(),
        P(),
    )
    out_specs = (P("seq", "mp"), P("seq", "mp"))
    return jax.shard_map(
        functools.partial(body, mesh.shape["seq"], mesh.shape["mp"]),
        mesh=mesh,
        in_specs=in_specs,
        out_specs=out_specs,
        check_vma=False,
    )
```

```python
import functools
import itertools

import jax
import jax.numpy as jnp
from jax import lax
from jax.experimental import pallas as pl
from jax.experimental.pallas import tpu as pltpu
from jax.sharding import PartitionSpec as P

MESH = pl.DeviceIdType.MESH
EPSILON = 1e-06
ROWS = 512
WIDTH = 512
LANES = 128
TAPS = 128
SHORT = 7
GSIZE = 16
PAD = 16
CHUNK = 64
TILE = 16
EXTRA = 4
F32 = jnp.float32
BF16 = jnp.bfloat16


def farthest_first(sizes, hops):
    offsets = list(itertools.product(*(range(size) for size in sizes)))[1:]
    way = lambda offset: sum(
        min(step, size - step) * hop for step, size, hop in zip(offset, sizes, hops)
    )
    return sorted(offsets, key=way, reverse=True)


def moved(index, sizes, offset):
    result, weight = 0, 1
    for size, step in zip(reversed(sizes), reversed(offset)):
        result = result + weight * lax.rem(lax.rem(index // weight, size) + step, size)
        weight *= size
    return result


def kernel(
    n_seq,
    n_mp,
    q_hbm,
    k_hbm,
    v_hbm,
    r_hbm,
    taps_hbm,
    filt_hbm,
    gain_hbm,
    pred_ref,
    len_ref,
    mixed_hbm,
    normed_hbm,
    qbuf,
    kbuf,
    vbuf,
    rbuf,
    tapsb,
    filtb,
    gainb,
    taps,
    qfeat,
    mix,
    msg,
    recv,
    fwd,
    fin,
    xmsg,
    xrecv,
    xfwd,
    xfin,
    rows_f,
    toep,
    flipped,
    summed,
    squares,
    mixed_v,
    normed_v,
    part,
    parts,
    load_sem,
    store_sem,
    send1,
    recv1,
    send2,
    recv2,
    send3,
    recv3,
    xsend1,
    xrecv1,
    xsend2,
    xrecv2,
):
    me = lax.axis_index("seq")
    mine = lax.axis_index("mp")

    body = pl.ds(PAD, ROWS)
    loads = [
        pltpu.make_async_copy(k_hbm, kbuf.at[body], load_sem.at[0]),
        pltpu.make_async_copy(v_hbm, vbuf.at[body], load_sem.at[1]),
        pltpu.make_async_copy(taps_hbm, tapsb, load_sem.at[2]),
        pltpu.make_async_copy(filt_hbm, filtb, load_sem.at[3]),
        pltpu.make_async_copy(q_hbm, qbuf.at[body], load_sem.at[4]),
        pltpu.make_async_copy(r_hbm, rbuf, load_sem.at[5]),
        pltpu.make_async_copy(gain_hbm, gainb, load_sem.at[6]),
    ]
    for load in loads:
        load.start()
    seq_parts, mp_parts = (n_seq // 2, 2), ((n_mp // 4, 2, 2) if n_mp % 4 == 0 else (n_mp,))
    seq_peers = [
        moved(me, seq_parts, offset) for offset in farthest_first(seq_parts, (1, 1))
    ]
    mp_peers = [
        moved(mine, mp_parts, offset)
        for offset in farthest_first(mp_parts, (2, 4, 1) if n_mp % 4 == 0 else (1,))
    ]
    barrier = pltpu.get_barrier_semaphore()
    for peer in seq_peers:
        pl.semaphore_signal(barrier, inc=1, device_id={"seq": peer}, device_id_type=MESH)
    for peer in mp_peers:
        pl.semaphore_signal(barrier, inc=1, device_id={"mp": peer}, device_id_type=MESH)

    def spread_out(source, landing, send_sem, recv_sem, peer):
        pltpu.make_async_remote_copy(
            src_ref=source,
            dst_ref=landing.at[me],
            send_sem=send_sem,
            recv_sem=recv_sem,
            device_id={"seq": peer},
            device_id_type=MESH,
        ).start()

    for ref in (qbuf, kbuf, vbuf):
        ref[0:PAD, :] = jnp.zeros((PAD, WIDTH), BF16)
    for load in loads[:4]:
        load.wait()
    for branch in range(3):
        taps[8 * branch : 8 * branch + SHORT, :] = tapsb[branch].astype(F32)

    def featurize(ref, branch, start, count, lanes):
        ext = ref[pl.ds(start, count + PAD), lanes].astype(F32)[PAD - 8 :]
        acc = taps[pl.ds(8 * branch, 1), lanes] * ext[8:]
        for s in range(1, SHORT):
            acc = acc + taps[pl.ds(8 * branch + s, 1), lanes] * pltpu.roll(ext, s, 0)[8:]
        return acc

    def product(start, count, lanes):
        key_feat = featurize(kbuf, 1, start, count, lanes)
        value_feat = featurize(vbuf, 2, start, count, lanes)
        return (key_feat * value_feat).astype(BF16)

    tiles = WIDTH // LANES
    per_tile = ROWS // CHUNK
    tail_chunks = TAPS // CHUNK

    def tail_step(c, _):
        for b in range(tiles):
            lanes = pl.ds(b * LANES, LANES)
            start = pl.multiple_of(ROWS - TAPS + c * CHUNK, CHUNK)
            value = product(start, CHUNK, lanes)
            mix[pl.ds(TAPS + start, CHUNK), lanes] = value
            for a in range(CHUNK // 16):
                msg[(c * (CHUNK // 16) + a) * tiles + b] = value[16 * a : 16 * a + 16]
        return 0

    lax.fori_loop(0, tail_chunks, tail_step, 0)

    pl.semaphore_wait(barrier, n_seq + n_mp - 2)
    for peer in seq_peers:
        spread_out(msg.at[peer], recv, send1, recv1, peer)
    recv[me] = msg[me]

    loads[4].wait()
    for i, ref in enumerate((qbuf, kbuf, vbuf)):
        tail = ref[PAD + ROWS - 16 : PAD + ROWS, :].astype(F32)[8:]
        for b in range(tiles):
            rows_f[pl.ds(4 * b + i, 8, stride=16), :] = tail[:, b * LANES : (b + 1) * LANES]
    filt = filtb[...].astype(F32)
    share, groups = filt.shape
    row = jnp.concatenate([filt[i : i + 1] for i in range(share)], axis=1)
    for b in range(tiles):
        rows_f[pl.ds(4 * b + 3, 8, stride=16), :] = jnp.broadcast_to(row, (8, LANES))

    def pack(p, _):
        xmsg[p] = rows_f[pl.ds(pl.multiple_of(4 * p, 4), 4), :].astype(BF16)
        return 0

    lax.fori_loop(0, n_seq, pack, 0)
    for peer in seq_peers:
        spread_out(xmsg.at[peer], xrecv, xsend1, xrecv1, peer)
    xrecv[me] = xmsg[me]

    def rest_step(c, _):
        start = pl.multiple_of(c * CHUNK, CHUNK)
        for b in range(tiles):
            lanes = pl.ds(b * LANES, LANES)
            mix[pl.ds(TAPS + start, CHUNK), lanes] = product(start, CHUNK, lanes)
        return 0

    lax.fori_loop(0, per_tile - tail_chunks, rest_step, 0)

    def query_step(c, _):
        start = pl.multiple_of(c * CHUNK, CHUNK)
        for b in range(tiles):
            lanes = pl.ds(b * LANES, LANES)
            qfeat[pl.ds(start, CHUNK), lanes] = featurize(qbuf, 0, start, CHUNK, lanes)
        return 0

    lax.fori_loop(0, per_tile, query_step, 0)
    squares[...] = jnp.zeros((ROWS, LANES), F32)

    others = pl.ds(0, n_seq - 1)
    pltpu.make_async_copy(recv.at[others], recv.at[others], recv1).wait()

    for peer in seq_peers:
        fwd[peer] = recv[jnp.maximum(pred_ref[peer], 0)]
        spread_out(fwd.at[peer], fin, send2, recv2, peer)
    fin[me] = recv[jnp.maximum(pred_ref[me], 0)]

    pltpu.make_async_copy(xrecv.at[others], xrecv.at[others], xrecv1).wait()
    for peer in seq_peers:
        xfwd[peer] = xrecv[jnp.maximum(pred_ref[peer], 0)]
        spread_out(xfwd.at[peer], xfin, xsend2, xrecv2, peer)
    xfin[me] = xrecv[jnp.maximum(pred_ref[me], 0)]

    def unpack_recv(p, _):
        rows_f[pl.ds(pl.multiple_of(4 * p, 4), 4), :] = xrecv[p].astype(F32)
        return 0

    lax.fori_loop(0, n_seq, unpack_recv, 0)
    gathered = rows_f[pl.ds(3, n_seq, stride=4), :]
    stacked = jnp.concatenate(
        [gathered[:, i * groups : (i + 1) * groups] for i in range(share)], axis=0
    )
    at = lax.broadcasted_iota(jnp.int32, (TAPS, LANES), 0)
    tap = share * (at & (n_seq - 1)) + at // n_seq
    place = (TAPS - tap) & (TAPS - 1)
    spread = (place == lax.broadcasted_iota(jnp.int32, (TAPS, LANES), 1)).astype(BF16)
    flipped[...] = lax.dot_general(
        stacked.astype(BF16), spread, (((0,), (0,)), ((), ())), preferred_element_type=F32
    )
    below = lax.broadcasted_iota(jnp.int32, (TAPS, LANES), 1) <= lax.broadcasted_iota(
        jnp.int32, (TAPS, LANES), 0
    )

    def toeplitz(g, _):
        first = jnp.broadcast_to(flipped[pl.ds(g, 1), :], (TAPS, LANES))
        turned = pltpu.roll(first, 0, 1, stride=1, stride_axis=0)
        rows = pl.ds(pl.multiple_of(g * TAPS, TAPS), TAPS)
        toep[rows, 0:LANES] = jnp.where(below, 0.0, turned).astype(BF16)
        toep[rows, LANES : 2 * LANES] = jnp.where(below, turned, 0.0).astype(BF16)
        return 0

    lax.fori_loop(0, groups, toeplitz, 0)

    length = len_ref[me]
    loads[5].wait()
    loads[6].wait()
    in_tile = LANES // GSIZE
    lane_group = lax.broadcasted_iota(jnp.int32, (TAPS, LANES), 1) // GSIZE

    def convolve(pair):
        def step(b, _):
            lanes = pl.ds(pl.multiple_of(b * LANES, LANES), LANES)
            window = jnp.concatenate(
                [mix[blk * TAPS : (blk + 2) * TAPS, lanes] for blk in pair], axis=1
            )
            rows = pl.ds(pl.multiple_of(b * in_tile * TAPS, TAPS), in_tile * TAPS)
            product_all = jnp.dot(toep[rows, :], window, preferred_element_type=F32)
            for half, blk in enumerate(pair):
                side = slice(half * LANES, (half + 1) * LANES)
                out = product_all[0:TAPS, side]
                for g in range(1, in_tile):
                    out = jnp.where(
                        lane_group == g, product_all[g * TAPS : (g + 1) * TAPS, side], out
                    )
                span = slice(blk * TAPS, (blk + 1) * TAPS)
                valid = (
                    lax.broadcasted_iota(jnp.int32, (TAPS, LANES), 0) + blk * TAPS
                ) < length
                mixed = jnp.where(valid, qfeat[span, lanes] * out, 0.0).astype(BF16)
                mixed_v[span, lanes] = mixed
                total = rbuf[span, lanes].astype(F32) + mixed.astype(F32)
                summed[span, lanes] = total
                squares[span, :] = squares[span, :] + total * total
            return 0

        lax.fori_loop(0, tiles, step, 0)

    def store_pair(pair, sem):
        span = pl.ds(pair[0] * TAPS, len(pair) * TAPS)
        return pltpu.make_async_copy(mixed_v.at[span], mixed_hbm.at[span], sem)

    convolve((2, 3))
    stores = [store_pair((2, 3), store_sem.at[0])]
    stores[0].start()

    pltpu.make_async_copy(fin.at[others], fin.at[others], recv2).wait()

    pltpu.make_async_copy(xfin.at[others], xfin.at[others], xrecv2).wait()
    keep = (pred_ref[me] >= 0).astype(F32)

    def unpack_fin(p, _):
        rows_f[pl.ds(pl.multiple_of(4 * p, 4), 4), :] = xfin[p].astype(F32) * keep
        return 0

    lax.fori_loop(0, n_seq, unpack_fin, 0)
    for a in range(TAPS // 16):
        for b in range(tiles):
            piece = (fin[a * tiles + b].astype(F32) * keep).astype(BF16)
            mix[16 * a : 16 * a + 16, b * LANES : (b + 1) * LANES] = piece
    for i, ref in enumerate((qbuf, kbuf, vbuf)):
        for b in range(tiles):
            head = rows_f[pl.ds(4 * b + i, 8, stride=16), :]
            ref[0:PAD, b * LANES : (b + 1) * LANES] = jnp.concatenate(
                [jnp.zeros_like(head), head], axis=0
            ).astype(BF16)
    for b in range(tiles):
        lanes = pl.ds(b * LANES, LANES)
        mix[TAPS : TAPS + 16, lanes] = product(0, 16, lanes)
        qfeat[0:16, lanes] = featurize(qbuf, 0, 0, 16, lanes)

    convolve((0, 1))
    stores.append(store_pair((0, 1), store_sem.at[1]))
    stores[1].start()

    for blk in range(ROWS // TAPS):
        span = slice(blk * TAPS, (blk + 1) * TAPS)
        part[:, span] = jnp.sum(squares[span, :].T, axis=0, keepdims=True)
    parts[mine] = part[...]

    for peer in mp_peers:
        pltpu.make_async_remote_copy(
            src_ref=part,
            dst_ref=parts.at[mine],
            send_sem=send3,
            recv_sem=recv3,
            device_id={"mp": peer},
            device_id_type=MESH,
        ).start()
    if n_mp > 1:
        peers = pl.ds(0, n_mp - 1)
        pltpu.make_async_copy(parts.at[peers], parts.at[peers], recv3).wait()
    total = jnp.sum(parts[...], axis=0)
    scale = lax.rsqrt(total / (WIDTH * n_mp) + EPSILON)
    gain = gainb[...].astype(F32).reshape(1, WIDTH)
    for blk in range(ROWS // TAPS):
        span = slice(blk * TAPS, (blk + 1) * TAPS)
        column = jnp.broadcast_to(scale[:, span], (TAPS, LANES)).T
        valid = (lax.broadcasted_iota(jnp.int32, (TAPS, LANES), 0) + blk * TAPS) < length
        for b in range(tiles):
            lanes = slice(b * LANES, (b + 1) * LANES)
            normed_v[span, lanes] = jnp.where(
                valid, summed[span, lanes] * column * gain[:, lanes], 0.0
            ).astype(BF16)
        part_rows = pl.ds(blk * TAPS, TAPS)
        stores.append(
            pltpu.make_async_copy(
                normed_v.at[part_rows], normed_hbm.at[part_rows], store_sem.at[2 + blk]
            )
        )
        stores[-1].start()

    pltpu.make_async_copy(msg.at[others], msg.at[others], send1).wait()
    pltpu.make_async_copy(fwd.at[others], fwd.at[others], send2).wait()
    pltpu.make_async_copy(xmsg.at[others], xmsg.at[others], xsend1).wait()
    pltpu.make_async_copy(xfwd.at[others], xfwd.at[others], xsend2).wait()
    if n_mp > 1:
        pltpu.make_async_copy(parts.at[peers], parts.at[peers], send3).wait()
    for store in stores:
        store.wait()


def body(n_seq, n_mp, queries, keys_in, values_in, residual, short_taps, mr_filter, norm_gain, predecessor, stretch_lengths):
    whole = pl.BlockSpec(memory_space=pltpu.HBM)
    scalars = pl.BlockSpec(memory_space=pltpu.SMEM)
    slots, extras = (n_seq, TILE, LANES), (n_seq, EXTRA, LANES)
    share, groups = mr_filter.shape
    out = jax.ShapeDtypeStruct((ROWS, WIDTH), BF16)
    return pl.pallas_call(
        functools.partial(kernel, n_seq, n_mp),
        out_shape=(out, out),
        in_specs=[whole] * 7 + [scalars] * 2,
        out_specs=(whole, whole),
        scratch_shapes=[
            pltpu.VMEM((PAD + ROWS, WIDTH), BF16),
            pltpu.VMEM((PAD + ROWS, WIDTH), BF16),
            pltpu.VMEM((PAD + ROWS, WIDTH), BF16),
            pltpu.VMEM((ROWS, WIDTH), BF16),
            pltpu.VMEM((3, SHORT, WIDTH), BF16),
            pltpu.VMEM((share, groups), BF16),
            pltpu.VMEM((WIDTH,), BF16),
            pltpu.VMEM((24, WIDTH), F32),
            pltpu.VMEM((ROWS, WIDTH), F32),
            pltpu.VMEM((TAPS + ROWS, WIDTH), BF16),
            *[pltpu.VMEM(slots, BF16)] * 4,
            *[pltpu.VMEM(extras, BF16)] * 4,
            pltpu.VMEM((LANES, LANES), F32),
            pltpu.VMEM((groups * TAPS, 2 * TAPS), BF16),
            pltpu.VMEM((groups, LANES), F32),
            pltpu.VMEM((ROWS, WIDTH), F32),
            pltpu.VMEM((ROWS, LANES), F32),
            pltpu.VMEM((ROWS, WIDTH), BF16),
            pltpu.VMEM((ROWS, WIDTH), BF16),
            pltpu.VMEM((1, ROWS), F32),
            pltpu.VMEM((n_mp, 1, ROWS), F32),
            pltpu.SemaphoreType.DMA((7,)),
            pltpu.SemaphoreType.DMA((6,)),
            *[pltpu.SemaphoreType.DMA] * 10,
        ],
        compiler_params=pltpu.CompilerParams(
            collective_id=0, has_side_effects=True, vmem_limit_bytes=58 * 1024 * 1024
        ),
    )(
        queries,
        keys_in,
        values_in,
        residual,
        short_taps,
        mr_filter,
        norm_gain,
        predecessor,
        stretch_lengths,
    )


def solution(mesh):
    in_specs = (
        P("seq", "mp"),
        P("seq", "mp"),
        P("seq", "mp"),
        P("seq", "mp"),
        P(None, None, "mp"),
        P("seq", "mp"),
        P("mp"),
        P(),
        P(),
    )
    out_specs = (P("seq", "mp"), P("seq", "mp"))
    return jax.shard_map(
        functools.partial(body, mesh.shape["seq"], mesh.shape["mp"]),
        mesh=mesh,
        in_specs=in_specs,
        out_specs=out_specs,
        check_vma=False,
    )
```

```python
import functools
import itertools

import jax
import jax.numpy as jnp
from jax import lax
from jax.experimental import pallas as pl
from jax.experimental.pallas import tpu as pltpu
from jax.sharding import PartitionSpec as P

MESH = pl.DeviceIdType.MESH
EPSILON = 1e-06
ROWS = 512
WIDTH = 512
LANES = 128
TAPS = 128
SHORT = 7
GSIZE = 16
PAD = 16
CHUNK = 64
TILE = 16
EXTRA = 4
LIMIT = 58 * 1024 * 1024
F32 = jnp.float32
BF16 = jnp.bfloat16


def farthest_first(sizes, hops):
    offsets = list(itertools.product(*(range(size) for size in sizes)))[1:]
    way = lambda offset: sum(
        min(step, size - step) * hop for step, size, hop in zip(offset, sizes, hops)
    )
    return sorted(offsets, key=way, reverse=True)


def moved(index, sizes, offset):
    result, weight = 0, 1
    for size, step in zip(reversed(sizes), reversed(offset)):
        result = result + weight * lax.rem(lax.rem(index // weight, size) + step, size)
        weight *= size
    return result


def kernel(
    n_seq,
    n_mp,
    q_hbm,
    k_hbm,
    v_hbm,
    r_hbm,
    taps_hbm,
    filt_hbm,
    gain_hbm,
    pred_ref,
    len_ref,
    mixed_v,
    rbuf,
    scale_ref,
    gain_ref,
    qbuf,
    kbuf,
    vbuf,
    tapsb,
    filtb,
    taps,
    qfeat,
    mix,
    msg,
    recv,
    fwd,
    fin,
    xmsg,
    xrecv,
    xfwd,
    xfin,
    rows_f,
    toep,
    flipped,
    squares,
    part,
    parts,
    load_sem,
    send1,
    recv1,
    send2,
    recv2,
    send3,
    recv3,
    xsend1,
    xrecv1,
    xsend2,
    xrecv2,
):
    me = lax.axis_index("seq")
    mine = lax.axis_index("mp")

    last = TAPS + PAD
    early, late = pl.ds(0, ROWS - last), pl.ds(ROWS - last, last)
    late_body, early_body = pl.ds(PAD + ROWS - last, last), pl.ds(PAD, ROWS - last)
    whole_body = pl.ds(PAD, ROWS)
    loads = [
        pltpu.make_async_copy(source, target, load_sem.at[i])
        for i, (source, target) in enumerate(
            (
                (taps_hbm, tapsb),
                (k_hbm.at[late], kbuf.at[late_body]),
                (v_hbm.at[late], vbuf.at[late_body]),
                (q_hbm, qbuf.at[whole_body]),
                (filt_hbm, filtb),
                (k_hbm.at[early], kbuf.at[early_body]),
                (v_hbm.at[early], vbuf.at[early_body]),
                (r_hbm, rbuf),
                (gain_hbm, gain_ref),
            )
        )
    ]
    for load in loads:
        load.start()
    seq_parts, mp_parts = (n_seq // 2, 2), ((n_mp // 4, 2, 2) if n_mp % 4 == 0 else (n_mp,))
    seq_peers = [
        moved(me, seq_parts, offset) for offset in farthest_first(seq_parts, (1, 1))
    ]
    mp_peers = [
        moved(mine, mp_parts, offset)
        for offset in farthest_first(mp_parts, (2, 4, 1) if n_mp % 4 == 0 else (1,))
    ]
    barrier = pltpu.get_barrier_semaphore()
    for peer in seq_peers:
        pl.semaphore_signal(barrier, inc=1, device_id={"seq": peer}, device_id_type=MESH)
    for peer in mp_peers:
        pl.semaphore_signal(barrier, inc=1, device_id={"mp": peer}, device_id_type=MESH)

    def spread_out(source, landing, send_sem, recv_sem, peer):
        pltpu.make_async_remote_copy(
            src_ref=source,
            dst_ref=landing.at[me],
            send_sem=send_sem,
            recv_sem=recv_sem,
            device_id={"seq": peer},
            device_id_type=MESH,
        ).start()

    for ref in (qbuf, kbuf, vbuf):
        ref[0:PAD, :] = jnp.zeros((PAD, WIDTH), BF16)
    for load in loads[:3]:
        load.wait()
    for branch in range(3):
        taps[8 * branch : 8 * branch + SHORT, :] = tapsb[branch].astype(F32)

    def featurize(ref, branch, start, count, lanes):
        ext = ref[pl.ds(start, count + PAD), lanes].astype(F32)[PAD - 8 :]
        acc = taps[pl.ds(8 * branch, 1), lanes] * ext[8:]
        for s in range(1, SHORT):
            acc = acc + taps[pl.ds(8 * branch + s, 1), lanes] * pltpu.roll(ext, s, 0)[8:]
        return acc

    def product(start, count, lanes):
        key_feat = featurize(kbuf, 1, start, count, lanes)
        value_feat = featurize(vbuf, 2, start, count, lanes)
        return (key_feat * value_feat).astype(BF16)

    tiles = WIDTH // LANES
    per_tile = ROWS // CHUNK
    tail_chunks = TAPS // CHUNK

    def tail_step(c, _):
        for b in range(tiles):
            lanes = pl.ds(b * LANES, LANES)
            start = pl.multiple_of(ROWS - TAPS + c * CHUNK, CHUNK)
            value = product(start, CHUNK, lanes)
            mix[pl.ds(TAPS + start, CHUNK), lanes] = value
            for a in range(CHUNK // 16):
                msg[(c * (CHUNK // 16) + a) * tiles + b] = value[16 * a : 16 * a + 16]
        return 0

    lax.fori_loop(0, tail_chunks, tail_step, 0)

    pl.semaphore_wait(barrier, n_seq + n_mp - 2)
    for peer in seq_peers:
        spread_out(msg.at[peer], recv, send1, recv1, peer)
    recv[me] = msg[me]

    loads[3].wait()
    loads[4].wait()
    for i, ref in enumerate((qbuf, kbuf, vbuf)):
        tail = ref[PAD + ROWS - 16 : PAD + ROWS, :].astype(F32)[8:]
        for b in range(tiles):
            rows_f[pl.ds(4 * b + i, 8, stride=16), :] = tail[:, b * LANES : (b + 1) * LANES]
    filt = filtb[...].astype(F32)
    share, groups = filt.shape
    row = jnp.concatenate([filt[i : i + 1] for i in range(share)], axis=1)
    for b in range(tiles):
        rows_f[pl.ds(4 * b + 3, 8, stride=16), :] = jnp.broadcast_to(row, (8, LANES))

    def pack(p, _):
        xmsg[p] = rows_f[pl.ds(pl.multiple_of(4 * p, 4), 4), :].astype(BF16)
        return 0

    lax.fori_loop(0, n_seq, pack, 0)
    for peer in seq_peers:
        spread_out(xmsg.at[peer], xrecv, xsend1, xrecv1, peer)
    xrecv[me] = xmsg[me]

    loads[5].wait()
    loads[6].wait()
    def rest_step(c, _):
        start = pl.multiple_of(c * CHUNK, CHUNK)
        for b in range(tiles):
            lanes = pl.ds(b * LANES, LANES)
            mix[pl.ds(TAPS + start, CHUNK), lanes] = product(start, CHUNK, lanes)
        return 0

    lax.fori_loop(0, per_tile - tail_chunks, rest_step, 0)

    def query_step(c, _):
        start = pl.multiple_of(c * CHUNK, CHUNK)
        for b in range(tiles):
            lanes = pl.ds(b * LANES, LANES)
            qfeat[pl.ds(start, CHUNK), lanes] = featurize(qbuf, 0, start, CHUNK, lanes)
        return 0

    lax.fori_loop(0, per_tile, query_step, 0)
    squares[...] = jnp.zeros((ROWS, LANES), F32)

    others = pl.ds(0, n_seq - 1)
    pltpu.make_async_copy(recv.at[others], recv.at[others], recv1).wait()

    for peer in seq_peers:
        fwd[peer] = recv[jnp.maximum(pred_ref[peer], 0)]
        spread_out(fwd.at[peer], fin, send2, recv2, peer)
    fin[me] = recv[jnp.maximum(pred_ref[me], 0)]

    pltpu.make_async_copy(xrecv.at[others], xrecv.at[others], xrecv1).wait()
    for peer in seq_peers:
        xfwd[peer] = xrecv[jnp.maximum(pred_ref[peer], 0)]
        spread_out(xfwd.at[peer], xfin, xsend2, xrecv2, peer)
    xfin[me] = xrecv[jnp.maximum(pred_ref[me], 0)]

    def unpack_recv(p, _):
        rows_f[pl.ds(pl.multiple_of(4 * p, 4), 4), :] = xrecv[p].astype(F32)
        return 0

    lax.fori_loop(0, n_seq, unpack_recv, 0)
    gathered = rows_f[pl.ds(3, n_seq, stride=4), :]
    stacked = jnp.concatenate(
        [gathered[:, i * groups : (i + 1) * groups] for i in range(share)], axis=0
    )
    at = lax.broadcasted_iota(jnp.int32, (TAPS, LANES), 0)
    tap = share * (at & (n_seq - 1)) + at // n_seq
    place = (TAPS - tap) & (TAPS - 1)
    spread = (place == lax.broadcasted_iota(jnp.int32, (TAPS, LANES), 1)).astype(BF16)
    flipped[...] = lax.dot_general(
        stacked.astype(BF16), spread, (((0,), (0,)), ((), ())), preferred_element_type=F32
    )
    below = lax.broadcasted_iota(jnp.int32, (TAPS, LANES), 1) <= lax.broadcasted_iota(
        jnp.int32, (TAPS, LANES), 0
    )

    def toeplitz(g, _):
        first = jnp.broadcast_to(flipped[pl.ds(g, 1), :], (TAPS, LANES))
        turned = pltpu.roll(first, 0, 1, stride=1, stride_axis=0)
        rows = pl.ds(pl.multiple_of(g * TAPS, TAPS), TAPS)
        toep[rows, 0:LANES] = jnp.where(below, 0.0, turned).astype(BF16)
        toep[rows, LANES : 2 * LANES] = jnp.where(below, turned, 0.0).astype(BF16)
        return 0

    lax.fori_loop(0, groups, toeplitz, 0)

    length = len_ref[me]
    loads[7].wait()
    loads[8].wait()
    in_tile = LANES // GSIZE
    lane_group = lax.broadcasted_iota(jnp.int32, (TAPS, LANES), 1) // GSIZE

    def convolve(pair):
        def step(b, _):
            lanes = pl.ds(pl.multiple_of(b * LANES, LANES), LANES)
            window = jnp.concatenate(
                [mix[blk * TAPS : (blk + 2) * TAPS, lanes] for blk in pair], axis=1
            )
            rows = pl.ds(pl.multiple_of(b * in_tile * TAPS, TAPS), in_tile * TAPS)
            product_all = jnp.dot(toep[rows, :], window, preferred_element_type=F32)
            for half, blk in enumerate(pair):
                side = slice(half * LANES, (half + 1) * LANES)
                out = product_all[0:TAPS, side]
                for g in range(1, in_tile):
                    out = jnp.where(
                        lane_group == g, product_all[g * TAPS : (g + 1) * TAPS, side], out
                    )
                span = slice(blk * TAPS, (blk + 1) * TAPS)
                valid = (
                    lax.broadcasted_iota(jnp.int32, (TAPS, LANES), 0) + blk * TAPS
                ) < length
                mixed = jnp.where(valid, qfeat[span, lanes] * out, 0.0).astype(BF16)
                mixed_v[span, lanes] = mixed
                total = rbuf[span, lanes].astype(F32) + mixed.astype(F32)
                squares[span, :] = squares[span, :] + total * total
            return 0

        lax.fori_loop(0, tiles, step, 0)

    convolve((2, 3))

    pltpu.make_async_copy(fin.at[others], fin.at[others], recv2).wait()

    pltpu.make_async_copy(xfin.at[others], xfin.at[others], xrecv2).wait()
    keep = (pred_ref[me] >= 0).astype(F32)

    def unpack_fin(p, _):
        rows_f[pl.ds(pl.multiple_of(4 * p, 4), 4), :] = xfin[p].astype(F32) * keep
        return 0

    lax.fori_loop(0, n_seq, unpack_fin, 0)
    for a in range(TAPS // 16):
        for b in range(tiles):
            piece = (fin[a * tiles + b].astype(F32) * keep).astype(BF16)
            mix[16 * a : 16 * a + 16, b * LANES : (b + 1) * LANES] = piece
    for i, ref in enumerate((qbuf, kbuf, vbuf)):
        for b in range(tiles):
            head = rows_f[pl.ds(4 * b + i, 8, stride=16), :]
            ref[0:PAD, b * LANES : (b + 1) * LANES] = jnp.concatenate(
                [jnp.zeros_like(head), head], axis=0
            ).astype(BF16)
    for b in range(tiles):
        lanes = pl.ds(b * LANES, LANES)
        mix[TAPS : TAPS + 16, lanes] = product(0, 16, lanes)
        qfeat[0:16, lanes] = featurize(qbuf, 0, 0, 16, lanes)

    convolve((0, 1))

    for blk in range(ROWS // TAPS):
        span = slice(blk * TAPS, (blk + 1) * TAPS)
        part[:, span] = jnp.sum(squares[span, :].T, axis=0, keepdims=True)
    parts[mine] = part[...]

    for peer in mp_peers:
        pltpu.make_async_remote_copy(
            src_ref=part,
            dst_ref=parts.at[mine],
            send_sem=send3,
            recv_sem=recv3,
            device_id={"mp": peer},
            device_id_type=MESH,
        ).start()
    if n_mp > 1:
        peers = pl.ds(0, n_mp - 1)
        pltpu.make_async_copy(parts.at[peers], parts.at[peers], recv3).wait()
    total = jnp.sum(parts[...], axis=0)
    token = lax.broadcasted_iota(jnp.int32, (1, ROWS), 1)
    scale = lax.rsqrt(total / (WIDTH * n_mp) + EPSILON)
    scale_ref[...] = jnp.where(token < length, scale, 0.0)

    pltpu.make_async_copy(msg.at[others], msg.at[others], send1).wait()
    pltpu.make_async_copy(fwd.at[others], fwd.at[others], send2).wait()
    pltpu.make_async_copy(xmsg.at[others], xmsg.at[others], xsend1).wait()
    pltpu.make_async_copy(xfwd.at[others], xfwd.at[others], xsend2).wait()
    if n_mp > 1:
        pltpu.make_async_copy(parts.at[peers], parts.at[peers], send3).wait()


def finish(gated, resid, scale_ref, gain_ref, mixed_hbm, normed_hbm, normed, sem):
    stores = [pltpu.make_async_copy(gated, mixed_hbm, sem.at[0])]
    stores[0].start()
    gain = gain_ref[...].astype(F32).reshape(1, WIDTH)
    for blk in range(ROWS // TAPS):
        rows = pl.ds(blk * TAPS, TAPS)
        factor = jnp.broadcast_to(scale_ref[:, blk * TAPS : (blk + 1) * TAPS], (TAPS, LANES)).T
        for b in range(WIDTH // LANES):
            lanes = slice(b * LANES, (b + 1) * LANES)
            total = resid[rows, lanes].astype(F32) + gated[rows, lanes].astype(F32)
            normed[rows, lanes] = (total * factor * gain[:, lanes]).astype(BF16)
        stores.append(
            pltpu.make_async_copy(normed.at[rows], normed_hbm.at[rows], sem.at[1 + blk])
        )
        stores[-1].start()
    for store in stores:
        store.wait()


def body(n_seq, n_mp, queries, keys_in, values_in, residual, short_taps, mr_filter, norm_gain, predecessor, stretch_lengths):
    whole = pl.BlockSpec(memory_space=pltpu.HBM)
    scalars = pl.BlockSpec(memory_space=pltpu.SMEM)
    slots, extras = (n_seq, TILE, LANES), (n_seq, EXTRA, LANES)
    share, groups = mr_filter.shape
    out = jax.ShapeDtypeStruct((ROWS, WIDTH), BF16)
    row = pl.BlockSpec(memory_space=pltpu.VMEM)
    gated, resid, scale, gain = pl.pallas_call(
        functools.partial(kernel, n_seq, n_mp),
        out_shape=(pltpu.VMEM((ROWS, WIDTH), BF16), pltpu.VMEM((ROWS, WIDTH), BF16), pltpu.VMEM((1, ROWS), F32), pltpu.VMEM((WIDTH,), BF16)),
        in_specs=[whole] * 7 + [scalars] * 2,
        out_specs=(row, row, row, row),
        scratch_shapes=[
            pltpu.VMEM((PAD + ROWS, WIDTH), BF16),
            pltpu.VMEM((PAD + ROWS, WIDTH), BF16),
            pltpu.VMEM((PAD + ROWS, WIDTH), BF16),
            pltpu.VMEM((3, SHORT, WIDTH), BF16),
            pltpu.VMEM((share, groups), BF16),
            pltpu.VMEM((24, WIDTH), F32),
            pltpu.VMEM((ROWS, WIDTH), F32),
            pltpu.VMEM((TAPS + ROWS, WIDTH), BF16),
            *[pltpu.VMEM(slots, BF16)] * 4,
            *[pltpu.VMEM(extras, BF16)] * 4,
            pltpu.VMEM((LANES, LANES), F32),
            pltpu.VMEM((groups * TAPS, 2 * TAPS), BF16),
            pltpu.VMEM((groups, LANES), F32),
            pltpu.VMEM((ROWS, LANES), F32),
            pltpu.VMEM((1, ROWS), F32),
            pltpu.VMEM((n_mp, 1, ROWS), F32),
            pltpu.SemaphoreType.DMA((9,)),
            *[pltpu.SemaphoreType.DMA] * 10,
        ],
        compiler_params=pltpu.CompilerParams(
            collective_id=0, has_side_effects=True, vmem_limit_bytes=LIMIT
        ),
    )(
        queries,
        keys_in,
        values_in,
        residual,
        short_taps,
        mr_filter,
        norm_gain,
        predecessor,
        stretch_lengths,
    )
    return pl.pallas_call(
        finish,
        out_shape=(out, out),
        in_specs=[row, row, row, row],
        out_specs=(whole, whole),
        scratch_shapes=[
            pltpu.VMEM((ROWS, WIDTH), BF16),
            pltpu.SemaphoreType.DMA((1 + ROWS // TAPS,)),
        ],
        compiler_params=pltpu.CompilerParams(vmem_limit_bytes=16 * 1024 * 1024),
    )(gated, resid, scale, gain)


def solution(mesh):
    in_specs = (
        P("seq", "mp"),
        P("seq", "mp"),
        P("seq", "mp"),
        P("seq", "mp"),
        P(None, None, "mp"),
        P("seq", "mp"),
        P("mp"),
        P(),
        P(),
    )
    out_specs = (P("seq", "mp"), P("seq", "mp"))
    return jax.shard_map(
        functools.partial(body, mesh.shape["seq"], mesh.shape["mp"]),
        mesh=mesh,
        in_specs=in_specs,
        out_specs=out_specs,
        check_vma=False,
    )
```

```python
import functools
import itertools

import jax
import jax.numpy as jnp
from jax import lax
from jax.experimental import pallas as pl
from jax.experimental.pallas import tpu as pltpu
from jax.sharding import PartitionSpec as P

MESH = pl.DeviceIdType.MESH
EPSILON = 1e-06
ROWS = 512
WIDTH = 512
LANES = 128
TAPS = 128
SHORT = 7
GSIZE = 16
PAD = 16
CHUNK = 64
QUAD = 4
TILE = 16
LIMIT = 58 * 1024 * 1024
F32 = jnp.float32
BF16 = jnp.bfloat16


def farthest_first(sizes, hops):
    offsets = list(itertools.product(*(range(size) for size in sizes)))[1:]
    way = lambda offset: sum(
        min(step, size - step) * hop for step, size, hop in zip(offset, sizes, hops)
    )
    return sorted(offsets, key=way, reverse=True)


def moved(index, sizes, offset):
    result, weight = 0, 1
    for size, step in zip(reversed(sizes), reversed(offset)):
        result = result + weight * lax.rem(lax.rem(index // weight, size) + step, size)
        weight *= size
    return result


def kernel(
    n_seq,
    n_mp,
    q_hbm,
    k_hbm,
    v_hbm,
    r_hbm,
    taps_hbm,
    filt_hbm,
    gain_hbm,
    pred_ref,
    len_ref,
    mixed_v,
    rbuf,
    scale_ref,
    gain_ref,
    qbuf,
    kbuf,
    vbuf,
    tapsb,
    filtb,
    taps,
    qfeat,
    mix,
    msg,
    recv,
    fwd,
    fin,
    rows_f,
    toep,
    flipped,
    squares,
    part,
    parts,
    load_sem,
    send1,
    recv1,
    send2,
    recv2,
    send3,
    recv3,
):
    me = lax.axis_index("seq")
    mine = lax.axis_index("mp")

    last = TAPS + PAD
    early, late = pl.ds(0, ROWS - last), pl.ds(ROWS - last, last)
    late_body, early_body = pl.ds(PAD + ROWS - last, last), pl.ds(PAD, ROWS - last)
    whole_body = pl.ds(PAD, ROWS)
    loads = [
        pltpu.make_async_copy(source, target, load_sem.at[i])
        for i, (source, target) in enumerate(
            (
                (taps_hbm, tapsb),
                (k_hbm.at[late], kbuf.at[late_body]),
                (v_hbm.at[late], vbuf.at[late_body]),
                (q_hbm, qbuf.at[whole_body]),
                (filt_hbm, filtb),
                (k_hbm.at[early], kbuf.at[early_body]),
                (v_hbm.at[early], vbuf.at[early_body]),
                (r_hbm, rbuf),
                (gain_hbm, gain_ref),
            )
        )
    ]
    for load in loads:
        load.start()
    seq_parts, mp_parts = (n_seq // 2, 2), ((n_mp // 4, 2, 2) if n_mp % 4 == 0 else (n_mp,))
    seq_peers = [
        moved(me, seq_parts, offset) for offset in farthest_first(seq_parts, (1, 1))
    ]
    mp_peers = [
        moved(mine, mp_parts, offset)
        for offset in farthest_first(mp_parts, (2, 4, 1) if n_mp % 4 == 0 else (1,))
    ]
    barrier = pltpu.get_barrier_semaphore()
    for peer in seq_peers:
        pl.semaphore_signal(barrier, inc=1, device_id={"seq": peer}, device_id_type=MESH)
    for peer in mp_peers:
        pl.semaphore_signal(barrier, inc=1, device_id={"mp": peer}, device_id_type=MESH)

    def spread_out(source, landing, send_sem, recv_sem, peer):
        pltpu.make_async_remote_copy(
            src_ref=source,
            dst_ref=landing.at[me],
            send_sem=send_sem,
            recv_sem=recv_sem,
            device_id={"seq": peer},
            device_id_type=MESH,
        ).start()

    for ref in (qbuf, kbuf, vbuf):
        ref[0:PAD, :] = jnp.zeros((PAD, WIDTH), BF16)
    for load in loads[:3]:
        load.wait()
    for branch in range(3):
        taps[8 * branch : 8 * branch + SHORT, :] = tapsb[branch].astype(F32)

    def featurize(ref, branch, start, count, lanes):
        ext = ref[pl.ds(start, count + PAD), lanes].astype(F32)[PAD - 8 :]
        acc = taps[pl.ds(8 * branch, 1), lanes] * ext[8:]
        for s in range(1, SHORT):
            acc = acc + taps[pl.ds(8 * branch + s, 1), lanes] * pltpu.roll(ext, s, 0)[8:]
        return acc

    def product(start, count, lanes):
        key_feat = featurize(kbuf, 1, start, count, lanes)
        value_feat = featurize(vbuf, 2, start, count, lanes)
        return (key_feat * value_feat).astype(BF16)

    tiles = WIDTH // LANES
    per_tile = ROWS // CHUNK
    tail_chunks = TAPS // CHUNK

    def tail_step(c, _):
        for b in range(tiles):
            lanes = pl.ds(b * LANES, LANES)
            start = pl.multiple_of(ROWS - TAPS + c * CHUNK, CHUNK)
            value = product(start, CHUNK, lanes)
            mix[pl.ds(TAPS + start, CHUNK), lanes] = value
            for a in range(CHUNK // TILE):
                p = (c * (CHUNK // TILE) + a) * tiles + b
                for i in range(TILE // QUAD):
                    first = TILE * a + QUAD * i
                    msg[p, i] = value[first : first + QUAD]
        return 0

    lax.fori_loop(0, tail_chunks, tail_step, 0)

    loads[3].wait()
    loads[4].wait()
    for i, ref in enumerate((qbuf, kbuf, vbuf)):
        tail = ref[PAD + ROWS - 16 : PAD + ROWS, :].astype(F32)[8:]
        for b in range(tiles):
            rows_f[pl.ds(4 * b + i, 8, stride=16), :] = tail[:, b * LANES : (b + 1) * LANES]
    filt = filtb[...].astype(F32)
    share, groups = filt.shape
    row = jnp.concatenate([filt[i : i + 1] for i in range(share)], axis=1)
    for b in range(tiles):
        rows_f[pl.ds(4 * b + 3, 8, stride=16), :] = jnp.broadcast_to(row, (8, LANES))

    def pack(p, _):
        msg[p, TILE // QUAD] = rows_f[pl.ds(pl.multiple_of(4 * p, 4), 4), :].astype(BF16)
        return 0

    lax.fori_loop(0, n_seq, pack, 0)
    pl.semaphore_wait(barrier, n_seq + n_mp - 2)
    for peer in seq_peers:
        spread_out(msg.at[peer], recv, send1, recv1, peer)
    recv[me] = msg[me]

    loads[5].wait()
    loads[6].wait()
    def rest_step(c, _):
        start = pl.multiple_of(c * CHUNK, CHUNK)
        for b in range(tiles):
            lanes = pl.ds(b * LANES, LANES)
            mix[pl.ds(TAPS + start, CHUNK), lanes] = product(start, CHUNK, lanes)
        return 0

    lax.fori_loop(0, per_tile - tail_chunks, rest_step, 0)

    def query_step(c, _):
        start = pl.multiple_of(c * CHUNK, CHUNK)
        for b in range(tiles):
            lanes = pl.ds(b * LANES, LANES)
            qfeat[pl.ds(start, CHUNK), lanes] = featurize(qbuf, 0, start, CHUNK, lanes)
        return 0

    lax.fori_loop(0, per_tile, query_step, 0)
    squares[...] = jnp.zeros((ROWS, LANES), F32)

    others = pl.ds(0, n_seq - 1)
    pltpu.make_async_copy(recv.at[others], recv.at[others], recv1).wait()

    for peer in seq_peers:
        fwd[peer] = recv[jnp.maximum(pred_ref[peer], 0)]
        spread_out(fwd.at[peer], fin, send2, recv2, peer)
    fin[me] = recv[jnp.maximum(pred_ref[me], 0)]

    def unpack_recv(p, _):
        rows_f[pl.ds(pl.multiple_of(4 * p, 4), 4), :] = recv[p, TILE // QUAD].astype(F32)
        return 0

    lax.fori_loop(0, n_seq, unpack_recv, 0)
    gathered = rows_f[pl.ds(3, n_seq, stride=4), :]
    stacked = jnp.concatenate(
        [gathered[:, i * groups : (i + 1) * groups] for i in range(share)], axis=0
    )
    at = lax.broadcasted_iota(jnp.int32, (TAPS, LANES), 0)
    tap = share * (at & (n_seq - 1)) + at // n_seq
    place = (TAPS - tap) & (TAPS - 1)
    spread = (place == lax.broadcasted_iota(jnp.int32, (TAPS, LANES), 1)).astype(BF16)
    flipped[...] = lax.dot_general(
        stacked.astype(BF16), spread, (((0,), (0,)), ((), ())), preferred_element_type=F32
    )
    below = lax.broadcasted_iota(jnp.int32, (TAPS, LANES), 1) <= lax.broadcasted_iota(
        jnp.int32, (TAPS, LANES), 0
    )

    def toeplitz(g, _):
        first = jnp.broadcast_to(flipped[pl.ds(g, 1), :], (TAPS, LANES))
        turned = pltpu.roll(first, 0, 1, stride=1, stride_axis=0)
        rows = pl.ds(pl.multiple_of(g * TAPS, TAPS), TAPS)
        toep[rows, 0:LANES] = jnp.where(below, 0.0, turned).astype(BF16)
        toep[rows, LANES : 2 * LANES] = jnp.where(below, turned, 0.0).astype(BF16)
        return 0

    lax.fori_loop(0, groups, toeplitz, 0)

    length = len_ref[me]
    loads[7].wait()
    loads[8].wait()
    in_tile = LANES // GSIZE
    lane_group = lax.broadcasted_iota(jnp.int32, (TAPS, LANES), 1) // GSIZE

    def convolve(pair):
        def step(b, _):
            lanes = pl.ds(pl.multiple_of(b * LANES, LANES), LANES)
            window = jnp.concatenate(
                [mix[blk * TAPS : (blk + 2) * TAPS, lanes] for blk in pair], axis=1
            )
            rows = pl.ds(pl.multiple_of(b * in_tile * TAPS, TAPS), in_tile * TAPS)
            product_all = jnp.dot(toep[rows, :], window, preferred_element_type=F32)
            for half, blk in enumerate(pair):
                side = slice(half * LANES, (half + 1) * LANES)
                out = product_all[0:TAPS, side]
                for g in range(1, in_tile):
                    out = jnp.where(
                        lane_group == g, product_all[g * TAPS : (g + 1) * TAPS, side], out
                    )
                span = slice(blk * TAPS, (blk + 1) * TAPS)
                valid = (
                    lax.broadcasted_iota(jnp.int32, (TAPS, LANES), 0) + blk * TAPS
                ) < length
                mixed = jnp.where(valid, qfeat[span, lanes] * out, 0.0).astype(BF16)
                mixed_v[span, lanes] = mixed
                total = rbuf[span, lanes].astype(F32) + mixed.astype(F32)
                squares[span, :] = squares[span, :] + total * total
            return 0

        lax.fori_loop(0, tiles, step, 0)

    convolve((2, 3))

    pltpu.make_async_copy(fin.at[others], fin.at[others], recv2).wait()

    keep = (pred_ref[me] >= 0).astype(F32)

    def unpack_fin(p, _):
        rows_f[pl.ds(pl.multiple_of(4 * p, 4), 4), :] = fin[p, TILE // QUAD].astype(F32) * keep
        return 0

    lax.fori_loop(0, n_seq, unpack_fin, 0)
    for a in range(TAPS // 16):
        for b in range(tiles):
            lanes = slice(b * LANES, (b + 1) * LANES)
            for i in range(TILE // QUAD):
                first = TILE * a + QUAD * i
                mix[first : first + QUAD, lanes] = fin[a * tiles + b, i]
    mix[0:TAPS, :] = (mix[0:TAPS, :].astype(F32) * keep).astype(BF16)
    for i, ref in enumerate((qbuf, kbuf, vbuf)):
        for b in range(tiles):
            head = rows_f[pl.ds(4 * b + i, 8, stride=16), :]
            ref[0:PAD, b * LANES : (b + 1) * LANES] = jnp.concatenate(
                [jnp.zeros_like(head), head], axis=0
            ).astype(BF16)
    for b in range(tiles):
        lanes = pl.ds(b * LANES, LANES)
        mix[TAPS : TAPS + 16, lanes] = product(0, 16, lanes)
        qfeat[0:16, lanes] = featurize(qbuf, 0, 0, 16, lanes)

    convolve((0, 1))

    for blk in range(ROWS // TAPS):
        span = slice(blk * TAPS, (blk + 1) * TAPS)
        part[:, span] = jnp.sum(squares[span, :].T, axis=0, keepdims=True)
    parts[mine] = part[...]

    for peer in mp_peers:
        pltpu.make_async_remote_copy(
            src_ref=part,
            dst_ref=parts.at[mine],
            send_sem=send3,
            recv_sem=recv3,
            device_id={"mp": peer},
            device_id_type=MESH,
        ).start()
    if n_mp > 1:
        peers = pl.ds(0, n_mp - 1)
        pltpu.make_async_copy(parts.at[peers], parts.at[peers], recv3).wait()
    total = jnp.sum(parts[...], axis=0)
    token = lax.broadcasted_iota(jnp.int32, (1, ROWS), 1)
    scale = lax.rsqrt(total / (WIDTH * n_mp) + EPSILON)
    scale_ref[...] = jnp.where(token < length, scale, 0.0)

    pltpu.make_async_copy(msg.at[others], msg.at[others], send1).wait()
    pltpu.make_async_copy(fwd.at[others], fwd.at[others], send2).wait()
    if n_mp > 1:
        pltpu.make_async_copy(parts.at[peers], parts.at[peers], send3).wait()


def finish(gated, resid, scale_ref, gain_ref, mixed_hbm, normed_hbm, normed, sem):
    stores = [pltpu.make_async_copy(gated, mixed_hbm, sem.at[0])]
    stores[0].start()
    gain = gain_ref[...].astype(F32).reshape(1, WIDTH)
    for blk in range(ROWS // TAPS):
        rows = pl.ds(blk * TAPS, TAPS)
        factor = jnp.broadcast_to(scale_ref[:, blk * TAPS : (blk + 1) * TAPS], (TAPS, LANES)).T
        for b in range(WIDTH // LANES):
            lanes = slice(b * LANES, (b + 1) * LANES)
            total = resid[rows, lanes].astype(F32) + gated[rows, lanes].astype(F32)
            normed[rows, lanes] = (total * factor * gain[:, lanes]).astype(BF16)
        stores.append(
            pltpu.make_async_copy(normed.at[rows], normed_hbm.at[rows], sem.at[1 + blk])
        )
        stores[-1].start()
    for store in stores:
        store.wait()


def body(n_seq, n_mp, queries, keys_in, values_in, residual, short_taps, mr_filter, norm_gain, predecessor, stretch_lengths):
    whole = pl.BlockSpec(memory_space=pltpu.HBM)
    scalars = pl.BlockSpec(memory_space=pltpu.SMEM)
    slots = (n_seq, TILE // QUAD + 1, QUAD, LANES)
    share, groups = mr_filter.shape
    out = jax.ShapeDtypeStruct((ROWS, WIDTH), BF16)
    row = pl.BlockSpec(memory_space=pltpu.VMEM)
    gated, resid, scale, gain = pl.pallas_call(
        functools.partial(kernel, n_seq, n_mp),
        out_shape=(pltpu.VMEM((ROWS, WIDTH), BF16), pltpu.VMEM((ROWS, WIDTH), BF16), pltpu.VMEM((1, ROWS), F32), pltpu.VMEM((WIDTH,), BF16)),
        in_specs=[whole] * 7 + [scalars] * 2,
        out_specs=(row, row, row, row),
        scratch_shapes=[
            pltpu.VMEM((PAD + ROWS, WIDTH), BF16),
            pltpu.VMEM((PAD + ROWS, WIDTH), BF16),
            pltpu.VMEM((PAD + ROWS, WIDTH), BF16),
            pltpu.VMEM((3, SHORT, WIDTH), BF16),
            pltpu.VMEM((share, groups), BF16),
            pltpu.VMEM((24, WIDTH), F32),
            pltpu.VMEM((ROWS, WIDTH), F32),
            pltpu.VMEM((TAPS + ROWS, WIDTH), BF16),
            *[pltpu.VMEM(slots, BF16)] * 4,
            pltpu.VMEM((LANES, LANES), F32),
            pltpu.VMEM((groups * TAPS, 2 * TAPS), BF16),
            pltpu.VMEM((groups, LANES), F32),
            pltpu.VMEM((ROWS, LANES), F32),
            pltpu.VMEM((1, ROWS), F32),
            pltpu.VMEM((n_mp, 1, ROWS), F32),
            pltpu.SemaphoreType.DMA((9,)),
            *[pltpu.SemaphoreType.DMA] * 6,
        ],
        compiler_params=pltpu.CompilerParams(
            collective_id=0, has_side_effects=True, vmem_limit_bytes=LIMIT
        ),
    )(
        queries,
        keys_in,
        values_in,
        residual,
        short_taps,
        mr_filter,
        norm_gain,
        predecessor,
        stretch_lengths,
    )
    return pl.pallas_call(
        finish,
        out_shape=(out, out),
        in_specs=[row, row, row, row],
        out_specs=(whole, whole),
        scratch_shapes=[
            pltpu.VMEM((ROWS, WIDTH), BF16),
            pltpu.SemaphoreType.DMA((1 + ROWS // TAPS,)),
        ],
        compiler_params=pltpu.CompilerParams(vmem_limit_bytes=16 * 1024 * 1024),
    )(gated, resid, scale, gain)


def solution(mesh):
    in_specs = (
        P("seq", "mp"),
        P("seq", "mp"),
        P("seq", "mp"),
        P("seq", "mp"),
        P(None, None, "mp"),
        P("seq", "mp"),
        P("mp"),
        P(),
        P(),
    )
    out_specs = (P("seq", "mp"), P("seq", "mp"))
    return jax.shard_map(
        functools.partial(body, mesh.shape["seq"], mesh.shape["mp"]),
        mesh=mesh,
        in_specs=in_specs,
        out_specs=out_specs,
        check_vma=False,
    )
```

```python
import functools
import itertools

import jax
import jax.numpy as jnp
from jax import lax
from jax.experimental import pallas as pl
from jax.experimental.pallas import tpu as pltpu
from jax.sharding import PartitionSpec as P

MESH = pl.DeviceIdType.MESH
EPSILON = 1e-06
ROWS = 512
WIDTH = 512
LANES = 128
TAPS = 128
SHORT = 7
GSIZE = 16
PAD = 16
CHUNK = 64
QUAD = 4
TILE = 16
LIMIT = 58 * 1024 * 1024
F32 = jnp.float32
BF16 = jnp.bfloat16


def farthest_first(sizes, hops):
    offsets = list(itertools.product(*(range(size) for size in sizes)))[1:]
    way = lambda offset: sum(
        min(step, size - step) * hop for step, size, hop in zip(offset, sizes, hops)
    )
    return sorted(offsets, key=way, reverse=True)


def moved(index, sizes, offset):
    result, weight = 0, 1
    for size, step in zip(reversed(sizes), reversed(offset)):
        result = result + weight * lax.rem(lax.rem(index // weight, size) + step, size)
        weight *= size
    return result


def kernel(
    n_seq,
    n_mp,
    q_hbm,
    k_hbm,
    v_hbm,
    r_hbm,
    taps_hbm,
    filt_hbm,
    gain_hbm,
    pred_ref,
    len_ref,
    mixed_v,
    rbuf,
    scale_ref,
    gain_ref,
    qbuf,
    kbuf,
    vbuf,
    tapsb,
    filtb,
    taps,
    qfeat,
    mix,
    msg,
    recv,
    fwd,
    fin,
    rows_f,
    toep,
    flipped,
    squares,
    seam,
    head_only,
    part,
    parts,
    load_sem,
    send1,
    recv1,
    send2,
    recv2,
    send3,
    recv3,
):
    me = lax.axis_index("seq")
    mine = lax.axis_index("mp")

    last = TAPS + PAD
    early, late = pl.ds(0, ROWS - last), pl.ds(ROWS - last, last)
    late_body, early_body = pl.ds(PAD + ROWS - last, last), pl.ds(PAD, ROWS - last)
    whole_body = pl.ds(PAD, ROWS)
    loads = [
        pltpu.make_async_copy(source, target, load_sem.at[i])
        for i, (source, target) in enumerate(
            (
                (taps_hbm, tapsb),
                (k_hbm.at[late], kbuf.at[late_body]),
                (v_hbm.at[late], vbuf.at[late_body]),
                (q_hbm, qbuf.at[whole_body]),
                (filt_hbm, filtb),
                (k_hbm.at[early], kbuf.at[early_body]),
                (v_hbm.at[early], vbuf.at[early_body]),
                (r_hbm, rbuf),
                (gain_hbm, gain_ref),
            )
        )
    ]
    for load in loads:
        load.start()
    seq_parts, mp_parts = (n_seq // 2, 2), ((n_mp // 4, 2, 2) if n_mp % 4 == 0 else (n_mp,))
    seq_peers = [
        moved(me, seq_parts, offset) for offset in farthest_first(seq_parts, (1, 1))
    ]
    mp_peers = [
        moved(mine, mp_parts, offset)
        for offset in farthest_first(mp_parts, (2, 4, 1) if n_mp % 4 == 0 else (1,))
    ]
    barrier = pltpu.get_barrier_semaphore()
    for peer in seq_peers:
        pl.semaphore_signal(barrier, inc=1, device_id={"seq": peer}, device_id_type=MESH)
    for peer in mp_peers:
        pl.semaphore_signal(barrier, inc=1, device_id={"mp": peer}, device_id_type=MESH)

    def spread_out(source, landing, send_sem, recv_sem, peer):
        pltpu.make_async_remote_copy(
            src_ref=source,
            dst_ref=landing.at[me],
            send_sem=send_sem,
            recv_sem=recv_sem,
            device_id={"seq": peer},
            device_id_type=MESH,
        ).start()

    for ref in (qbuf, kbuf, vbuf):
        ref[0:PAD, :] = jnp.zeros((PAD, WIDTH), BF16)
    for load in loads[:3]:
        load.wait()
    for branch in range(3):
        taps[8 * branch : 8 * branch + SHORT, :] = tapsb[branch].astype(F32)

    def featurize(ref, branch, start, count, lanes):
        ext = ref[pl.ds(start, count + PAD), lanes].astype(F32)[PAD - 8 :]
        acc = taps[pl.ds(8 * branch, 1), lanes] * ext[8:]
        for s in range(1, SHORT):
            acc = acc + taps[pl.ds(8 * branch + s, 1), lanes] * pltpu.roll(ext, s, 0)[8:]
        return acc

    def product(start, count, lanes):
        key_feat = featurize(kbuf, 1, start, count, lanes)
        value_feat = featurize(vbuf, 2, start, count, lanes)
        return (key_feat * value_feat).astype(BF16)

    tiles = WIDTH // LANES
    per_tile = ROWS // CHUNK
    tail_chunks = TAPS // CHUNK

    def tail_step(c, _):
        for b in range(tiles):
            lanes = pl.ds(b * LANES, LANES)
            start = pl.multiple_of(ROWS - TAPS + c * CHUNK, CHUNK)
            value = product(start, CHUNK, lanes)
            mix[pl.ds(TAPS + start, CHUNK), lanes] = value
            for a in range(CHUNK // TILE):
                p = (c * (CHUNK // TILE) + a) * tiles + b
                for i in range(TILE // QUAD):
                    first = TILE * a + QUAD * i
                    msg[p, i] = value[first : first + QUAD]
        return 0

    lax.fori_loop(0, tail_chunks, tail_step, 0)

    loads[3].wait()
    loads[4].wait()
    for i, ref in enumerate((qbuf, kbuf, vbuf)):
        tail = ref[PAD + ROWS - 16 : PAD + ROWS, :].astype(F32)[8:]
        for b in range(tiles):
            rows_f[pl.ds(4 * b + i, 8, stride=16), :] = tail[:, b * LANES : (b + 1) * LANES]
    filt = filtb[...].astype(F32)
    share, groups = filt.shape
    row = jnp.concatenate([filt[i : i + 1] for i in range(share)], axis=1)
    for b in range(tiles):
        rows_f[pl.ds(4 * b + 3, 8, stride=16), :] = jnp.broadcast_to(row, (8, LANES))

    def pack(p, _):
        msg[p, TILE // QUAD] = rows_f[pl.ds(pl.multiple_of(4 * p, 4), 4), :].astype(BF16)
        return 0

    lax.fori_loop(0, n_seq, pack, 0)
    pl.semaphore_wait(barrier, n_seq + n_mp - 2)
    for peer in seq_peers:
        spread_out(msg.at[peer], recv, send1, recv1, peer)
    recv[me] = msg[me]

    loads[5].wait()
    loads[6].wait()
    def rest_step(c, _):
        start = pl.multiple_of(c * CHUNK, CHUNK)
        for b in range(tiles):
            lanes = pl.ds(b * LANES, LANES)
            mix[pl.ds(TAPS + start, CHUNK), lanes] = product(start, CHUNK, lanes)
        return 0

    lax.fori_loop(0, per_tile - tail_chunks, rest_step, 0)

    def query_step(c, _):
        start = pl.multiple_of(c * CHUNK, CHUNK)
        for b in range(tiles):
            lanes = pl.ds(b * LANES, LANES)
            qfeat[pl.ds(start, CHUNK), lanes] = featurize(qbuf, 0, start, CHUNK, lanes)
        return 0

    lax.fori_loop(0, per_tile, query_step, 0)
    squares[...] = jnp.zeros((ROWS, LANES), F32)

    others = pl.ds(0, n_seq - 1)
    pltpu.make_async_copy(recv.at[others], recv.at[others], recv1).wait()

    for peer in seq_peers:
        fwd[peer] = recv[jnp.maximum(pred_ref[peer], 0)]
        spread_out(fwd.at[peer], fin, send2, recv2, peer)
    fin[me] = recv[jnp.maximum(pred_ref[me], 0)]

    def unpack_recv(p, _):
        rows_f[pl.ds(pl.multiple_of(4 * p, 4), 4), :] = recv[p, TILE // QUAD].astype(F32)
        return 0

    lax.fori_loop(0, n_seq, unpack_recv, 0)
    gathered = rows_f[pl.ds(3, n_seq, stride=4), :]
    stacked = jnp.concatenate(
        [gathered[:, i * groups : (i + 1) * groups] for i in range(share)], axis=0
    )
    at = lax.broadcasted_iota(jnp.int32, (TAPS, LANES), 0)
    tap = share * (at & (n_seq - 1)) + at // n_seq
    place = (TAPS - tap) & (TAPS - 1)
    spread = (place == lax.broadcasted_iota(jnp.int32, (TAPS, LANES), 1)).astype(BF16)
    flipped[...] = lax.dot_general(
        stacked.astype(BF16), spread, (((0,), (0,)), ((), ())), preferred_element_type=F32
    )
    below = lax.broadcasted_iota(jnp.int32, (TAPS, LANES), 1) <= lax.broadcasted_iota(
        jnp.int32, (TAPS, LANES), 0
    )

    def toeplitz(g, _):
        first = jnp.broadcast_to(flipped[pl.ds(g, 1), :], (TAPS, LANES))
        turned = pltpu.roll(first, 0, 1, stride=1, stride_axis=0)
        rows = pl.ds(pl.multiple_of(g * TAPS, TAPS), TAPS)
        toep[rows, 0:LANES] = jnp.where(below, 0.0, turned).astype(BF16)
        toep[rows, LANES : 2 * LANES] = jnp.where(below, turned, 0.0).astype(BF16)
        return 0

    lax.fori_loop(0, groups, toeplitz, 0)

    length = len_ref[me]
    loads[7].wait()
    loads[8].wait()
    in_tile = LANES // GSIZE
    lane_group = lax.broadcasted_iota(jnp.int32, (TAPS, LANES), 1) // GSIZE

    def chosen(stack, count):
        out = stack[0:count]
        for g in range(1, in_tile):
            own = lane_group[0:count] == g
            out = jnp.where(own, stack[g * count : (g + 1) * count], out)
        return out

    def gate(start, count, lanes, out):
        rows = pl.ds(start, count)
        valid = (lax.broadcasted_iota(jnp.int32, (count, LANES), 0) + start) < length
        mixed = jnp.where(valid, qfeat[rows, lanes] * out, 0.0).astype(BF16)
        mixed_v[rows, lanes] = mixed
        total = rbuf[rows, lanes].astype(F32) + mixed.astype(F32)
        return total * total

    def convolve(blocks, unroll=False):
        def step(b, _):
            lanes = pl.ds(b * LANES if unroll else pl.multiple_of(b * LANES, LANES), LANES)
            windows = [mix[blk * TAPS : (blk + 2) * TAPS, lanes] for blk in blocks]
            first = b * in_tile * TAPS
            rows = pl.ds(first if unroll else pl.multiple_of(first, TAPS), in_tile * TAPS)
            window = jnp.concatenate(windows, axis=1)
            product_all = jnp.concatenate([jnp.dot(
                toep[pl.ds(first + g * TAPS, TAPS), :], window, preferred_element_type=F32
            ) for g in range(in_tile)], axis=0)
            for half, blk in enumerate(blocks):
                out = chosen(product_all[:, half * LANES : (half + 1) * LANES], TAPS)
                if blk == 1:
                    seam[:, lanes] = out[0:16]
                span = slice(blk * TAPS, (blk + 1) * TAPS)
                squares[span, :] = squares[span, :] + gate(blk * TAPS, TAPS, lanes, out)
            return 0

        if unroll:
            for b in range(tiles):
                step(b, 0)
        else:
            lax.fori_loop(0, tiles, step, 0)

    def row_of_sums(blk):
        span = slice(blk * TAPS, (blk + 1) * TAPS)
        part[:, span] = jnp.sum(squares[span, :].T, axis=0, keepdims=True)

    mix[TAPS : TAPS + 16, :] = jnp.zeros((16, WIDTH), BF16)
    head_only[...] = jnp.zeros((TAPS, WIDTH), BF16)
    convolve((1,))
    convolve((2, 3))
    row_of_sums(2)
    row_of_sums(3)

    pltpu.make_async_copy(fin.at[others], fin.at[others], recv2).wait()

    keep = (pred_ref[me] >= 0).astype(F32)

    for p in range(n_seq):
        rows_f[QUAD * p : QUAD * (p + 1), :] = fin[p, TILE // QUAD].astype(F32) * keep
    for a in range(TAPS // 16):
        for b in range(tiles):
            lanes = slice(b * LANES, (b + 1) * LANES)
            for i in range(TILE // QUAD):
                first = TILE * a + QUAD * i
                mix[first : first + QUAD, lanes] = fin[a * tiles + b, i]
    mix[0:TAPS, :] = (mix[0:TAPS, :].astype(F32) * keep).astype(BF16)
    for i, ref in enumerate((qbuf, kbuf, vbuf)):
        for b in range(tiles):
            head = rows_f[pl.ds(4 * b + i, 8, stride=16), :]
            ref[0:PAD, b * LANES : (b + 1) * LANES] = jnp.concatenate(
                [jnp.zeros_like(head), head], axis=0
            ).astype(BF16)
    for b in range(tiles):
        lanes = pl.ds(b * LANES, LANES)
        head = product(0, 16, lanes)
        mix[TAPS : TAPS + 16, lanes] = head
        head_only[0:16, lanes] = head
        qfeat[0:16, lanes] = featurize(qbuf, 0, 0, 16, lanes)

    seam_squares = jnp.zeros((16, LANES), F32)
    for b in range(tiles):
        lanes = pl.ds(b * LANES, LANES)
        firsts = [
            toep[(b * in_tile + g) * TAPS : (b * in_tile + g) * TAPS + 16, 0:TAPS]
            for g in range(in_tile)
        ]
        added = jnp.dot(
            jnp.concatenate(firsts, axis=0), head_only[:, lanes], preferred_element_type=F32
        )
        out = seam[:, lanes] + chosen(added, 16)
        seam_squares = seam_squares + gate(TAPS, 16, lanes, out)
    squares[TAPS : TAPS + 16, :] = seam_squares

    convolve((0,), unroll=True)
    row_of_sums(0)
    row_of_sums(1)
    parts[mine] = part[...]

    for peer in mp_peers:
        pltpu.make_async_remote_copy(
            src_ref=part,
            dst_ref=parts.at[mine],
            send_sem=send3,
            recv_sem=recv3,
            device_id={"mp": peer},
            device_id_type=MESH,
        ).start()
    if n_mp > 1:
        peers = pl.ds(0, n_mp - 1)
        pltpu.make_async_copy(parts.at[peers], parts.at[peers], recv3).wait()
    total = jnp.sum(parts[...], axis=0)
    token = lax.broadcasted_iota(jnp.int32, (1, ROWS), 1)
    scale = lax.rsqrt(total / (WIDTH * n_mp) + EPSILON)
    scale_ref[...] = jnp.where(token < length, scale, 0.0)

    pltpu.make_async_copy(msg.at[others], msg.at[others], send1).wait()
    pltpu.make_async_copy(fwd.at[others], fwd.at[others], send2).wait()
    if n_mp > 1:
        pltpu.make_async_copy(parts.at[peers], parts.at[peers], send3).wait()


def finish(gated, resid, scale_ref, gain_ref, mixed_hbm, normed_hbm, normed, sem):
    stores = [pltpu.make_async_copy(gated, mixed_hbm, sem.at[0])]
    stores[0].start()
    gain = gain_ref[...].astype(F32).reshape(1, WIDTH)
    for blk in range(ROWS // TAPS):
        rows = pl.ds(blk * TAPS, TAPS)
        factor = jnp.broadcast_to(scale_ref[:, blk * TAPS : (blk + 1) * TAPS], (TAPS, LANES)).T
        for b in range(WIDTH // LANES):
            lanes = slice(b * LANES, (b + 1) * LANES)
            total = resid[rows, lanes].astype(F32) + gated[rows, lanes].astype(F32)
            normed[rows, lanes] = (total * factor * gain[:, lanes]).astype(BF16)
        stores.append(
            pltpu.make_async_copy(normed.at[rows], normed_hbm.at[rows], sem.at[1 + blk])
        )
        stores[-1].start()
    for store in stores:
        store.wait()


def body(n_seq, n_mp, queries, keys_in, values_in, residual, short_taps, mr_filter, norm_gain, predecessor, stretch_lengths):
    whole = pl.BlockSpec(memory_space=pltpu.HBM)
    scalars = pl.BlockSpec(memory_space=pltpu.SMEM)
    slots = (n_seq, TILE // QUAD + 1, QUAD, LANES)
    share, groups = mr_filter.shape
    out = jax.ShapeDtypeStruct((ROWS, WIDTH), BF16)
    row = pl.BlockSpec(memory_space=pltpu.VMEM)
    gated, resid, scale, gain = pl.pallas_call(
        functools.partial(kernel, n_seq, n_mp),
        out_shape=(pltpu.VMEM((ROWS, WIDTH), BF16), pltpu.VMEM((ROWS, WIDTH), BF16), pltpu.VMEM((1, ROWS), F32), pltpu.VMEM((WIDTH,), BF16)),
        in_specs=[whole] * 7 + [scalars] * 2,
        out_specs=(row, row, row, row),
        scratch_shapes=[
            pltpu.VMEM((PAD + ROWS, WIDTH), BF16),
            pltpu.VMEM((PAD + ROWS, WIDTH), BF16),
            pltpu.VMEM((PAD + ROWS, WIDTH), BF16),
            pltpu.VMEM((3, SHORT, WIDTH), BF16),
            pltpu.VMEM((share, groups), BF16),
            pltpu.VMEM((24, WIDTH), F32),
            pltpu.VMEM((ROWS, WIDTH), F32),
            pltpu.VMEM((TAPS + ROWS, WIDTH), BF16),
            *[pltpu.VMEM(slots, BF16)] * 4,
            pltpu.VMEM((LANES, LANES), F32),
            pltpu.VMEM((groups * TAPS, 2 * TAPS), BF16),
            pltpu.VMEM((groups, LANES), F32),
            pltpu.VMEM((ROWS, LANES), F32),
            pltpu.VMEM((16, WIDTH), F32),
            pltpu.VMEM((TAPS, WIDTH), BF16),
            pltpu.VMEM((1, ROWS), F32),
            pltpu.VMEM((n_mp, 1, ROWS), F32),
            pltpu.SemaphoreType.DMA((9,)),
            *[pltpu.SemaphoreType.DMA] * 6,
        ],
        compiler_params=pltpu.CompilerParams(
            collective_id=0, has_side_effects=True, vmem_limit_bytes=LIMIT
        ),
    )(
        queries,
        keys_in,
        values_in,
        residual,
        short_taps,
        mr_filter,
        norm_gain,
        predecessor,
        stretch_lengths,
    )
    return pl.pallas_call(
        finish,
        out_shape=(out, out),
        in_specs=[row, row, row, row],
        out_specs=(whole, whole),
        scratch_shapes=[
            pltpu.VMEM((ROWS, WIDTH), BF16),
            pltpu.SemaphoreType.DMA((1 + ROWS // TAPS,)),
        ],
        compiler_params=pltpu.CompilerParams(vmem_limit_bytes=16 * 1024 * 1024),
    )(gated, resid, scale, gain)


def solution(mesh):
    in_specs = (
        P("seq", "mp"),
        P("seq", "mp"),
        P("seq", "mp"),
        P("seq", "mp"),
        P(None, None, "mp"),
        P("seq", "mp"),
        P("mp"),
        P(),
        P(),
    )
    out_specs = (P("seq", "mp"), P("seq", "mp"))
    return jax.shard_map(
        functools.partial(body, mesh.shape["seq"], mesh.shape["mp"]),
        mesh=mesh,
        in_specs=in_specs,
        out_specs=out_specs,
        check_vma=False,
    )
```

```python
import functools
import itertools

import jax
import jax.numpy as jnp
from jax import lax
from jax.experimental import pallas as pl
from jax.experimental.pallas import tpu as pltpu
from jax.sharding import PartitionSpec as P

MESH = pl.DeviceIdType.MESH
EPSILON = 1e-06
ROWS = 512
WIDTH = 512
LANES = 128
TAPS = 128
SHORT = 7
GSIZE = 16
PAD = 16
CHUNK = 64
QUAD = 4
TILE = 16
LIMIT = 58 * 1024 * 1024
F32 = jnp.float32
BF16 = jnp.bfloat16


def farthest_first(sizes, hops):
    offsets = list(itertools.product(*(range(size) for size in sizes)))[1:]
    way = lambda offset: sum(
        min(step, size - step) * hop for step, size, hop in zip(offset, sizes, hops)
    )
    return sorted(offsets, key=way, reverse=True)


def moved(index, sizes, offset):
    result, weight = 0, 1
    for size, step in zip(reversed(sizes), reversed(offset)):
        result = result + weight * lax.rem(lax.rem(index // weight, size) + step, size)
        weight *= size
    return result


def kernel(
    n_seq,
    n_mp,
    q_hbm,
    k_hbm,
    v_hbm,
    r_hbm,
    taps_hbm,
    filt_hbm,
    gain_hbm,
    pred_ref,
    len_ref,
    mixed_v,
    rbuf,
    scale_ref,
    gain_ref,
    qbuf,
    kbuf,
    vbuf,
    tapsb,
    filtb,
    taps,
    qfeat,
    mix,
    msg,
    recv,
    fwd,
    fin,
    rows_f,
    toep,
    flipped,
    squares,
    seam,
    head_only,
    part,
    parts,
    load_sem,
    send1,
    recv1,
    send2,
    recv2,
    send3,
    recv3,
):
    me = lax.axis_index("seq")
    mine = lax.axis_index("mp")

    last = TAPS + PAD
    early, late = pl.ds(0, ROWS - last), pl.ds(ROWS - last, last)
    late_body, early_body = pl.ds(PAD + ROWS - last, last), pl.ds(PAD, ROWS - last)
    whole_body = pl.ds(PAD, ROWS)
    loads = [
        pltpu.make_async_copy(source, target, load_sem.at[i])
        for i, (source, target) in enumerate(
            (
                (taps_hbm, tapsb),
                (k_hbm.at[late], kbuf.at[late_body]),
                (v_hbm.at[late], vbuf.at[late_body]),
                (q_hbm, qbuf.at[whole_body]),
                (filt_hbm, filtb),
                (k_hbm.at[early], kbuf.at[early_body]),
                (v_hbm.at[early], vbuf.at[early_body]),
                (r_hbm, rbuf),
                (gain_hbm, gain_ref),
            )
        )
    ]
    seq_parts, mp_parts = (n_seq // 2, 2), ((n_mp // 4, 2, 2) if n_mp % 4 == 0 else (n_mp,))
    seq_peers = [
        moved(me, seq_parts, offset) for offset in farthest_first(seq_parts, (1, 1))
    ]
    mp_peers = [
        moved(mine, mp_parts, offset)
        for offset in farthest_first(mp_parts, (2, 4, 1) if n_mp % 4 == 0 else (1,))
    ]
    barrier = pltpu.get_barrier_semaphore()
    for peer in seq_peers[:15]:
        pl.semaphore_signal(barrier, inc=1, device_id={"seq": peer}, device_id_type=MESH)
    for peer in mp_peers:
        pl.semaphore_signal(barrier, inc=1, device_id={"mp": peer}, device_id_type=MESH)
    for peer in seq_peers[15:]:
        pl.semaphore_signal(barrier, inc=1, device_id={"seq": peer}, device_id_type=MESH)
    for load in loads:
        load.start()

    def spread_out(source, landing, send_sem, recv_sem, peer):
        pltpu.make_async_remote_copy(
            src_ref=source,
            dst_ref=landing.at[me],
            send_sem=send_sem,
            recv_sem=recv_sem,
            device_id={"seq": peer},
            device_id_type=MESH,
        ).start()

    for ref in (qbuf, kbuf, vbuf):
        ref[0:PAD, :] = jnp.zeros((PAD, WIDTH), BF16)
    for load in loads[:3]:
        load.wait()
    for branch in range(3):
        taps[8 * branch : 8 * branch + SHORT, :] = tapsb[branch].astype(F32)

    def featurize(ref, branch, start, count, lanes):
        ext = ref[pl.ds(start, count + PAD), lanes].astype(F32)[PAD - 8 :]
        acc = taps[pl.ds(8 * branch, 1), lanes] * ext[8:]
        for s in range(1, SHORT):
            acc = acc + taps[pl.ds(8 * branch + s, 1), lanes] * pltpu.roll(ext, s, 0)[8:]
        return acc

    def product(start, count, lanes):
        key_feat = featurize(kbuf, 1, start, count, lanes)
        value_feat = featurize(vbuf, 2, start, count, lanes)
        return (key_feat * value_feat).astype(BF16)

    tiles = WIDTH // LANES
    per_tile = ROWS // CHUNK
    tail_chunks = TAPS // CHUNK

    def tail_step(c, _):
        for b in range(tiles):
            lanes = pl.ds(b * LANES, LANES)
            start = pl.multiple_of(ROWS - TAPS + c * CHUNK, CHUNK)
            value = product(start, CHUNK, lanes)
            mix[pl.ds(TAPS + start, CHUNK), lanes] = value
            for a in range(CHUNK // TILE):
                p = (c * (CHUNK // TILE) + a) * tiles + b
                for i in range(TILE // QUAD):
                    first = TILE * a + QUAD * i
                    msg[p, i] = value[first : first + QUAD]
        return 0

    lax.fori_loop(0, tail_chunks, tail_step, 0)

    loads[3].wait()
    loads[4].wait()
    for i, ref in enumerate((qbuf, kbuf, vbuf)):
        tail = ref[PAD + ROWS - 16 : PAD + ROWS, :].astype(F32)[8:]
        for b in range(tiles):
            rows_f[pl.ds(4 * b + i, 8, stride=16), :] = tail[:, b * LANES : (b + 1) * LANES]
    filt = filtb[...].astype(F32)
    share, groups = filt.shape
    row = jnp.concatenate([filt[i : i + 1] for i in range(share)], axis=1)
    for b in range(tiles):
        rows_f[pl.ds(4 * b + 3, 8, stride=16), :] = jnp.broadcast_to(row, (8, LANES))

    def pack(p, _):
        msg[p, TILE // QUAD] = rows_f[pl.ds(pl.multiple_of(4 * p, 4), 4), :].astype(BF16)
        return 0

    lax.fori_loop(0, n_seq, pack, 0)
    pl.semaphore_wait(barrier, n_seq + n_mp - 2)
    for peer in seq_peers:
        spread_out(msg.at[peer], recv, send1, recv1, peer)
    recv[me] = msg[me]

    loads[5].wait()
    loads[6].wait()
    def rest_step(c, _):
        start = pl.multiple_of(c * CHUNK, CHUNK)
        for b in range(tiles):
            lanes = pl.ds(b * LANES, LANES)
            mix[pl.ds(TAPS + start, CHUNK), lanes] = product(start, CHUNK, lanes)
        return 0

    lax.fori_loop(0, per_tile - tail_chunks, rest_step, 0)

    def query_step(c, _):
        start = pl.multiple_of(c * CHUNK, CHUNK)
        for b in range(tiles):
            lanes = pl.ds(b * LANES, LANES)
            qfeat[pl.ds(start, CHUNK), lanes] = featurize(qbuf, 0, start, CHUNK, lanes)
        return 0

    lax.fori_loop(0, per_tile, query_step, 0)
    squares[...] = jnp.zeros((ROWS, LANES), F32)

    others = pl.ds(0, n_seq - 1)
    pltpu.make_async_copy(recv.at[others], recv.at[others], recv1).wait()

    for peer in seq_peers:
        fwd[peer] = recv[jnp.maximum(pred_ref[peer], 0)]
        spread_out(fwd.at[peer], fin, send2, recv2, peer)
    fin[me] = recv[jnp.maximum(pred_ref[me], 0)]

    def unpack_recv(p, _):
        rows_f[pl.ds(pl.multiple_of(4 * p, 4), 4), :] = recv[p, TILE // QUAD].astype(F32)
        return 0

    lax.fori_loop(0, n_seq, unpack_recv, 0)
    gathered = rows_f[pl.ds(3, n_seq, stride=4), :]
    stacked = jnp.concatenate(
        [gathered[:, i * groups : (i + 1) * groups] for i in range(share)], axis=0
    )
    at = lax.broadcasted_iota(jnp.int32, (TAPS, LANES), 0)
    tap = share * (at & (n_seq - 1)) + at // n_seq
    place = (TAPS - tap) & (TAPS - 1)
    spread = (place == lax.broadcasted_iota(jnp.int32, (TAPS, LANES), 1)).astype(BF16)
    flipped[...] = lax.dot_general(
        stacked.astype(BF16), spread, (((0,), (0,)), ((), ())), preferred_element_type=F32
    )
    below = lax.broadcasted_iota(jnp.int32, (TAPS, LANES), 1) <= lax.broadcasted_iota(
        jnp.int32, (TAPS, LANES), 0
    )

    def toeplitz(g, _):
        first = jnp.broadcast_to(flipped[pl.ds(g, 1), :], (TAPS, LANES))
        turned = pltpu.roll(first, 0, 1, stride=1, stride_axis=0)
        rows = pl.ds(pl.multiple_of(g * TAPS, TAPS), TAPS)
        toep[rows, 0:LANES] = jnp.where(below, 0.0, turned).astype(BF16)
        toep[rows, LANES : 2 * LANES] = jnp.where(below, turned, 0.0).astype(BF16)
        return 0

    lax.fori_loop(0, groups, toeplitz, 0)

    length = len_ref[me]
    loads[7].wait()
    loads[8].wait()
    in_tile = LANES // GSIZE
    lane_group = lax.broadcasted_iota(jnp.int32, (TAPS, LANES), 1) // GSIZE

    def chosen(stack, count):
        out = stack[0:count]
        for g in range(1, in_tile):
            own = lane_group[0:count] == g
            out = jnp.where(own, stack[g * count : (g + 1) * count], out)
        return out

    def gate(start, count, lanes, out):
        rows = pl.ds(start, count)
        valid = (lax.broadcasted_iota(jnp.int32, (count, LANES), 0) + start) < length
        mixed = jnp.where(valid, qfeat[rows, lanes] * out, 0.0).astype(BF16)
        mixed_v[rows, lanes] = mixed
        total = rbuf[rows, lanes].astype(F32) + mixed.astype(F32)
        return total * total

    def convolve(blocks, unroll=False):
        def step(b, _):
            lanes = pl.ds(b * LANES if unroll else pl.multiple_of(b * LANES, LANES), LANES)
            windows = [mix[blk * TAPS : (blk + 2) * TAPS, lanes] for blk in blocks]
            first = b * in_tile * TAPS
            rows = pl.ds(first if unroll else pl.multiple_of(first, TAPS), in_tile * TAPS)
            window = jnp.concatenate(windows, axis=1)
            product_all = jnp.concatenate([jnp.dot(
                toep[pl.ds(first + g * TAPS, TAPS), :], window, preferred_element_type=F32
            ) for g in range(in_tile)], axis=0)
            for half, blk in enumerate(blocks):
                out = chosen(product_all[:, half * LANES : (half + 1) * LANES], TAPS)
                if blk == 1:
                    seam[:, lanes] = out[0:16]
                span = slice(blk * TAPS, (blk + 1) * TAPS)
                squares[span, :] = squares[span, :] + gate(blk * TAPS, TAPS, lanes, out)
            return 0

        if unroll:
            for b in range(tiles):
                step(b, 0)
        else:
            lax.fori_loop(0, tiles, step, 0)

    def row_of_sums(blk):
        span = slice(blk * TAPS, (blk + 1) * TAPS)
        part[:, span] = jnp.sum(squares[span, :].T, axis=0, keepdims=True)

    mix[TAPS : TAPS + 16, :] = jnp.zeros((16, WIDTH), BF16)
    head_only[...] = jnp.zeros((TAPS, WIDTH), BF16)
    convolve((1,))
    convolve((2, 3))
    row_of_sums(2)
    row_of_sums(3)

    pltpu.make_async_copy(fin.at[others], fin.at[others], recv2).wait()

    keep = (pred_ref[me] >= 0).astype(F32)

    for p in range(n_seq):
        rows_f[QUAD * p : QUAD * (p + 1), :] = fin[p, TILE // QUAD].astype(F32) * keep
    for a in range(TAPS // 16):
        for b in range(tiles):
            lanes = slice(b * LANES, (b + 1) * LANES)
            for i in range(TILE // QUAD):
                first = TILE * a + QUAD * i
                mix[first : first + QUAD, lanes] = fin[a * tiles + b, i]
    mix[0:TAPS, :] = (mix[0:TAPS, :].astype(F32) * keep).astype(BF16)
    for i, ref in enumerate((qbuf, kbuf, vbuf)):
        for b in range(tiles):
            head = rows_f[pl.ds(4 * b + i, 8, stride=16), :]
            ref[0:PAD, b * LANES : (b + 1) * LANES] = jnp.concatenate(
                [jnp.zeros_like(head), head], axis=0
            ).astype(BF16)
    for b in range(tiles):
        lanes = pl.ds(b * LANES, LANES)
        head = product(0, 16, lanes)
        mix[TAPS : TAPS + 16, lanes] = head
        head_only[0:16, lanes] = head
        qfeat[0:16, lanes] = featurize(qbuf, 0, 0, 16, lanes)

    seam_squares = jnp.zeros((16, LANES), F32)
    for b in range(tiles):
        lanes = pl.ds(b * LANES, LANES)
        firsts = [
            toep[(b * in_tile + g) * TAPS : (b * in_tile + g) * TAPS + 16, 0:TAPS]
            for g in range(in_tile)
        ]
        added = jnp.dot(
            jnp.concatenate(firsts, axis=0), head_only[:, lanes], preferred_element_type=F32
        )
        out = seam[:, lanes] + chosen(added, 16)
        seam_squares = seam_squares + gate(TAPS, 16, lanes, out)
    squares[TAPS : TAPS + 16, :] = seam_squares

    convolve((0,), unroll=True)
    row_of_sums(0)
    row_of_sums(1)
    parts[mine] = part[...]

    for peer in mp_peers:
        pltpu.make_async_remote_copy(
            src_ref=part,
            dst_ref=parts.at[mine],
            send_sem=send3,
            recv_sem=recv3,
            device_id={"mp": peer},
            device_id_type=MESH,
        ).start()
    if n_mp > 1:
        peers = pl.ds(0, n_mp - 1)
        pltpu.make_async_copy(parts.at[peers], parts.at[peers], recv3).wait()
    total = jnp.sum(parts[...], axis=0)
    token = lax.broadcasted_iota(jnp.int32, (1, ROWS), 1)
    scale = lax.rsqrt(total / (WIDTH * n_mp) + EPSILON)
    scale_ref[...] = jnp.where(token < length, scale, 0.0)

    pltpu.make_async_copy(msg.at[others], msg.at[others], send1).wait()
    pltpu.make_async_copy(fwd.at[others], fwd.at[others], send2).wait()
    if n_mp > 1:
        pltpu.make_async_copy(parts.at[peers], parts.at[peers], send3).wait()


def finish(gated, resid, scale_ref, gain_ref, mixed_hbm, normed_hbm, normed, sem):
    stores = [pltpu.make_async_copy(gated, mixed_hbm, sem.at[0])]
    stores[0].start()
    gain = gain_ref[...].astype(F32).reshape(1, WIDTH)
    for blk in range(ROWS // TAPS):
        rows = pl.ds(blk * TAPS, TAPS)
        factor = jnp.broadcast_to(scale_ref[:, blk * TAPS : (blk + 1) * TAPS], (TAPS, LANES)).T
        for b in range(WIDTH // LANES):
            lanes = slice(b * LANES, (b + 1) * LANES)
            total = resid[rows, lanes].astype(F32) + gated[rows, lanes].astype(F32)
            normed[rows, lanes] = (total * factor * gain[:, lanes]).astype(BF16)
        stores.append(
            pltpu.make_async_copy(normed.at[rows], normed_hbm.at[rows], sem.at[1 + blk])
        )
        stores[-1].start()
    for store in stores:
        store.wait()


def body(n_seq, n_mp, queries, keys_in, values_in, residual, short_taps, mr_filter, norm_gain, predecessor, stretch_lengths):
    whole = pl.BlockSpec(memory_space=pltpu.HBM)
    scalars = pl.BlockSpec(memory_space=pltpu.SMEM)
    slots = (n_seq, TILE // QUAD + 1, QUAD, LANES)
    share, groups = mr_filter.shape
    out = jax.ShapeDtypeStruct((ROWS, WIDTH), BF16)
    row = pl.BlockSpec(memory_space=pltpu.VMEM)
    gated, resid, scale, gain = pl.pallas_call(
        functools.partial(kernel, n_seq, n_mp),
        out_shape=(pltpu.VMEM((ROWS, WIDTH), BF16), pltpu.VMEM((ROWS, WIDTH), BF16), pltpu.VMEM((1, ROWS), F32), pltpu.VMEM((WIDTH,), BF16)),
        in_specs=[whole] * 7 + [scalars] * 2,
        out_specs=(row, row, row, row),
        scratch_shapes=[
            pltpu.VMEM((PAD + ROWS, WIDTH), BF16),
            pltpu.VMEM((PAD + ROWS, WIDTH), BF16),
            pltpu.VMEM((PAD + ROWS, WIDTH), BF16),
            pltpu.VMEM((3, SHORT, WIDTH), BF16),
            pltpu.VMEM((share, groups), BF16),
            pltpu.VMEM((24, WIDTH), F32),
            pltpu.VMEM((ROWS, WIDTH), F32),
            pltpu.VMEM((TAPS + ROWS, WIDTH), BF16),
            *[pltpu.VMEM(slots, BF16)] * 4,
            pltpu.VMEM((LANES, LANES), F32),
            pltpu.VMEM((groups * TAPS, 2 * TAPS), BF16),
            pltpu.VMEM((groups, LANES), F32),
            pltpu.VMEM((ROWS, LANES), F32),
            pltpu.VMEM((16, WIDTH), F32),
            pltpu.VMEM((TAPS, WIDTH), BF16),
            pltpu.VMEM((1, ROWS), F32),
            pltpu.VMEM((n_mp, 1, ROWS), F32),
            pltpu.SemaphoreType.DMA((9,)),
            *[pltpu.SemaphoreType.DMA] * 6,
        ],
        compiler_params=pltpu.CompilerParams(
            collective_id=0, has_side_effects=True, vmem_limit_bytes=LIMIT
        ),
    )(
        queries,
        keys_in,
        values_in,
        residual,
        short_taps,
        mr_filter,
        norm_gain,
        predecessor,
        stretch_lengths,
    )
    return pl.pallas_call(
        finish,
        out_shape=(out, out),
        in_specs=[row, row, row, row],
        out_specs=(whole, whole),
        scratch_shapes=[
            pltpu.VMEM((ROWS, WIDTH), BF16),
            pltpu.SemaphoreType.DMA((1 + ROWS // TAPS,)),
        ],
        compiler_params=pltpu.CompilerParams(vmem_limit_bytes=16 * 1024 * 1024),
    )(gated, resid, scale, gain)


def solution(mesh):
    in_specs = (
        P("seq", "mp"),
        P("seq", "mp"),
        P("seq", "mp"),
        P("seq", "mp"),
        P(None, None, "mp"),
        P("seq", "mp"),
        P("mp"),
        P(),
        P(),
    )
    out_specs = (P("seq", "mp"), P("seq", "mp"))
    return jax.shard_map(
        functools.partial(body, mesh.shape["seq"], mesh.shape["mp"]),
        mesh=mesh,
        in_specs=in_specs,
        out_specs=out_specs,
        check_vma=False,
    )
```

```python
import functools
import itertools

import jax
import jax.numpy as jnp
from jax import lax
from jax.experimental import pallas as pl
from jax.experimental.pallas import tpu as pltpu
from jax.sharding import PartitionSpec as P

MESH = pl.DeviceIdType.MESH
EPSILON = 1e-06
ROWS = 512
WIDTH = 512
LANES = 128
TAPS = 128
SHORT = 7
GSIZE = 16
PAD = 16
CHUNK = 64
QUAD = 4
TILE = 16
LIMIT = 58 * 1024 * 1024
F32 = jnp.float32
BF16 = jnp.bfloat16


def farthest_first(sizes, hops):
    offsets = list(itertools.product(*(range(size) for size in sizes)))[1:]
    way = lambda offset: sum(
        min(step, size - step) * hop for step, size, hop in zip(offset, sizes, hops)
    )
    return sorted(offsets, key=way, reverse=True)


def moved(index, sizes, offset):
    result, weight = 0, 1
    for size, step in zip(reversed(sizes), reversed(offset)):
        result = result + weight * lax.rem(lax.rem(index // weight, size) + step, size)
        weight *= size
    return result


def kernel(
    n_seq,
    n_mp,
    q_hbm,
    k_hbm,
    v_hbm,
    r_hbm,
    taps_hbm,
    filt_hbm,
    gain_hbm,
    pred_ref,
    len_ref,
    mixed_v,
    rbuf,
    scale_ref,
    gain_ref,
    qbuf,
    kbuf,
    vbuf,
    tapsb,
    filtb,
    taps,
    qfeat,
    mix,
    msg,
    recv,
    fwd,
    fin,
    rows_f,
    toep,
    flipped,
    squares,
    seam,
    head_only,
    part,
    parts,
    load_sem,
    send1,
    recv1,
    send2,
    recv2,
    send3,
    recv3,
):
    me = lax.axis_index("seq")
    mine = lax.axis_index("mp")

    last = TAPS + PAD
    early, late = pl.ds(0, ROWS - last), pl.ds(ROWS - last, last)
    late_body, early_body = pl.ds(PAD + ROWS - last, last), pl.ds(PAD, ROWS - last)
    whole_body = pl.ds(PAD, ROWS)
    loads = [
        pltpu.make_async_copy(source, target, load_sem.at[i])
        for i, (source, target) in enumerate(
            (
                (taps_hbm, tapsb),
                (k_hbm.at[late], kbuf.at[late_body]),
                (v_hbm.at[late], vbuf.at[late_body]),
                (q_hbm, qbuf.at[whole_body]),
                (filt_hbm, filtb),
                (k_hbm.at[early], kbuf.at[early_body]),
                (v_hbm.at[early], vbuf.at[early_body]),
                (r_hbm, rbuf),
                (gain_hbm, gain_ref),
            )
        )
    ]
    seq_parts, mp_parts = (n_seq // 2, 2), ((n_mp // 4, 2, 2) if n_mp % 4 == 0 else (n_mp,))
    seq_peers = [
        moved(me, seq_parts, offset) for offset in farthest_first(seq_parts, (1, 1))
    ]
    mp_peers = [
        moved(mine, mp_parts, offset)
        for offset in farthest_first(mp_parts, (2, 4, 1) if n_mp % 4 == 0 else (1,))
    ]
    barrier = pltpu.get_barrier_semaphore()
    for peer in seq_peers[:15]:
        pl.semaphore_signal(barrier, inc=1, device_id={"seq": peer}, device_id_type=MESH)
    for peer in mp_peers:
        pl.semaphore_signal(barrier, inc=1, device_id={"mp": peer}, device_id_type=MESH)
    for peer in seq_peers[15:]:
        pl.semaphore_signal(barrier, inc=1, device_id={"seq": peer}, device_id_type=MESH)
    for load in loads:
        load.start()

    def spread_out(source, landing, send_sem, recv_sem, peer):
        pltpu.make_async_remote_copy(
            src_ref=source,
            dst_ref=landing.at[me],
            send_sem=send_sem,
            recv_sem=recv_sem,
            device_id={"seq": peer},
            device_id_type=MESH,
        ).start()

    for ref in (qbuf, kbuf, vbuf):
        ref[0:PAD, :] = jnp.zeros((PAD, WIDTH), BF16)
    for load in loads[:3]:
        load.wait()
    for branch in range(3):
        taps[8 * branch : 8 * branch + SHORT, :] = tapsb[branch].astype(F32)

    def featurize(ref, branch, start, count, lanes):
        ext = ref[pl.ds(start, count + PAD), lanes].astype(F32)[PAD - 8 :]
        acc = taps[pl.ds(8 * branch, 1), lanes] * ext[8:]
        for s in range(1, SHORT):
            acc = acc + taps[pl.ds(8 * branch + s, 1), lanes] * pltpu.roll(ext, s, 0)[8:]
        return acc

    def product(start, count, lanes):
        key_feat = featurize(kbuf, 1, start, count, lanes)
        value_feat = featurize(vbuf, 2, start, count, lanes)
        return (key_feat * value_feat).astype(BF16)

    tiles = WIDTH // LANES
    per_tile = ROWS // CHUNK
    tail_chunks = TAPS // CHUNK

    def tail_step(c, _):
        for b in range(tiles):
            lanes = pl.ds(b * LANES, LANES)
            start = pl.multiple_of(ROWS - TAPS + c * CHUNK, CHUNK)
            value = product(start, CHUNK, lanes)
            mix[pl.ds(TAPS + start, CHUNK), lanes] = value
            for a in range(CHUNK // TILE):
                p = (c * (CHUNK // TILE) + a) * tiles + b
                for i in range(TILE // QUAD):
                    first = TILE * a + QUAD * i
                    msg[p, i] = value[first : first + QUAD]
        return 0

    lax.fori_loop(0, tail_chunks, tail_step, 0)

    loads[3].wait()
    loads[4].wait()
    for i, ref in enumerate((qbuf, kbuf, vbuf)):
        tail = ref[PAD + ROWS - 16 : PAD + ROWS, :].astype(F32)[8:]
        for b in range(tiles):
            rows_f[pl.ds(4 * b + i, 8, stride=16), :] = tail[:, b * LANES : (b + 1) * LANES]
    filt = filtb[...].astype(F32)
    share, groups = filt.shape
    row = jnp.concatenate([filt[i : i + 1] for i in range(share)], axis=1)
    for b in range(tiles):
        rows_f[pl.ds(4 * b + 3, 8, stride=16), :] = jnp.broadcast_to(row, (8, LANES))

    def pack(p, _):
        msg[p, TILE // QUAD] = rows_f[pl.ds(pl.multiple_of(4 * p, 4), 4), :].astype(BF16)
        return 0

    lax.fori_loop(0, n_seq, pack, 0)
    pl.semaphore_wait(barrier, n_seq + n_mp - 2)
    for peer in seq_peers:
        spread_out(msg.at[peer], recv, send1, recv1, peer)
    recv[me] = msg[me]

    loads[5].wait()
    loads[6].wait()
    def rest_step(c, _):
        start = pl.multiple_of(c * CHUNK, CHUNK)
        for b in range(tiles):
            lanes = pl.ds(b * LANES, LANES)
            mix[pl.ds(TAPS + start, CHUNK), lanes] = product(start, CHUNK, lanes)
        return 0

    lax.fori_loop(0, per_tile - tail_chunks, rest_step, 0)

    def query_step(c, _):
        start = pl.multiple_of(c * CHUNK, CHUNK)
        for b in range(tiles):
            lanes = pl.ds(b * LANES, LANES)
            qfeat[pl.ds(start, CHUNK), lanes] = featurize(qbuf, 0, start, CHUNK, lanes)
        return 0

    lax.fori_loop(0, per_tile, query_step, 0)
    squares[...] = jnp.zeros((ROWS, LANES), F32)

    others = pl.ds(0, n_seq - 1)
    pltpu.make_async_copy(recv.at[others], recv.at[others], recv1).wait()

    for peer in seq_peers:
        fwd[peer] = recv[jnp.maximum(pred_ref[peer], 0)]
        spread_out(fwd.at[peer], fin, send2, recv2, peer)
    fin[me] = recv[jnp.maximum(pred_ref[me], 0)]

    def unpack_recv(p, _):
        rows_f[pl.ds(pl.multiple_of(4 * p, 4), 4), :] = recv[p, TILE // QUAD].astype(F32)
        return 0

    lax.fori_loop(0, n_seq, unpack_recv, 0)
    gathered = rows_f[pl.ds(3, n_seq, stride=4), :]
    stacked = jnp.concatenate(
        [gathered[:, i * groups : (i + 1) * groups] for i in range(share)], axis=0
    )
    at = lax.broadcasted_iota(jnp.int32, (TAPS, LANES), 0)
    tap = share * (at & (n_seq - 1)) + at // n_seq
    place = (TAPS - tap) & (TAPS - 1)
    spread = (place == lax.broadcasted_iota(jnp.int32, (TAPS, LANES), 1)).astype(BF16)
    flipped[...] = lax.dot_general(
        stacked.astype(BF16), spread, (((0,), (0,)), ((), ())), preferred_element_type=F32
    )
    below = lax.broadcasted_iota(jnp.int32, (TAPS, LANES), 1) <= lax.broadcasted_iota(
        jnp.int32, (TAPS, LANES), 0
    )

    def toeplitz(g, _):
        first = jnp.broadcast_to(flipped[pl.ds(g, 1), :], (TAPS, LANES))
        turned = pltpu.roll(first, 0, 1, stride=1, stride_axis=0)
        rows = pl.ds(pl.multiple_of(g * TAPS, TAPS), TAPS)
        toep[rows, 0:LANES] = jnp.where(below, 0.0, turned).astype(BF16)
        toep[rows, LANES : 2 * LANES] = jnp.where(below, turned, 0.0).astype(BF16)
        return 0

    lax.fori_loop(0, groups, toeplitz, 0)

    length = len_ref[me]
    loads[7].wait()
    loads[8].wait()
    in_tile = LANES // GSIZE
    lane_group = lax.broadcasted_iota(jnp.int32, (TAPS, LANES), 1) // GSIZE

    def chosen(stack, count):
        out = stack[0:count]
        for g in range(1, in_tile):
            own = lane_group[0:count] == g
            out = jnp.where(own, stack[g * count : (g + 1) * count], out)
        return out

    def gate(start, count, lanes, out):
        rows = pl.ds(start, count)
        valid = (lax.broadcasted_iota(jnp.int32, (count, LANES), 0) + start) < length
        mixed = jnp.where(valid, qfeat[rows, lanes] * out, 0.0).astype(BF16)
        mixed_v[rows, lanes] = mixed
        total = rbuf[rows, lanes].astype(F32) + mixed.astype(F32)
        return total * total

    def convolve(blocks, unroll=False):
        def step(b, _):
            lanes = pl.ds(b * LANES if unroll else pl.multiple_of(b * LANES, LANES), LANES)
            windows = [mix[blk * TAPS : (blk + 2) * TAPS, lanes] for blk in blocks]
            first = b * in_tile * TAPS
            rows = pl.ds(first if unroll else pl.multiple_of(first, TAPS), in_tile * TAPS)
            window = jnp.concatenate(windows, axis=1)
            product_all = jnp.concatenate([jnp.dot(
                toep[pl.ds(first + g * TAPS, TAPS), :], window, preferred_element_type=F32
            ) for g in range(in_tile)], axis=0)
            for half, blk in enumerate(blocks):
                out = chosen(product_all[:, half * LANES : (half + 1) * LANES], TAPS)
                if blk == 1:
                    seam[:, lanes] = out[0:16]
                span = slice(blk * TAPS, (blk + 1) * TAPS)
                squares[span, :] = squares[span, :] + gate(blk * TAPS, TAPS, lanes, out)
            return 0

        if unroll:
            for b in range(tiles):
                step(b, 0)
        else:
            lax.fori_loop(0, tiles, step, 0)

    def row_of_sums(blk):
        span = slice(blk * TAPS, (blk + 1) * TAPS)
        part[:, span] = jnp.sum(squares[span, :].T, axis=0, keepdims=True)

    mix[TAPS : TAPS + 16, :] = jnp.zeros((16, WIDTH), BF16)
    head_only[...] = jnp.zeros((TAPS, WIDTH), BF16)
    convolve((1,))
    convolve((2, 3))
    row_of_sums(2)
    row_of_sums(3)

    pltpu.make_async_copy(fin.at[others], fin.at[others], recv2).wait()

    keep = (pred_ref[me] >= 0).astype(F32)

    for p in range(n_seq):
        rows_f[QUAD * p : QUAD * (p + 1), :] = fin[p, TILE // QUAD].astype(F32) * keep
    for a in range(TAPS // 16):
        for b in range(tiles):
            lanes = slice(b * LANES, (b + 1) * LANES)
            for i in range(TILE // QUAD):
                first = TILE * a + QUAD * i
                mix[first : first + QUAD, lanes] = fin[a * tiles + b, i]
    mix[0:TAPS, :] = (mix[0:TAPS, :].astype(F32) * keep).astype(BF16)
    for i, ref in enumerate((qbuf, kbuf, vbuf)):
        for b in range(tiles):
            head = rows_f[pl.ds(4 * b + i, 8, stride=16), :]
            ref[0:PAD, b * LANES : (b + 1) * LANES] = jnp.concatenate(
                [jnp.zeros_like(head), head], axis=0
            ).astype(BF16)
    for b in range(tiles):
        lanes = pl.ds(b * LANES, LANES)
        head = product(0, 16, lanes)
        mix[TAPS : TAPS + 16, lanes] = head
        head_only[0:16, lanes] = head
        qfeat[0:16, lanes] = featurize(qbuf, 0, 0, 16, lanes)

    convolve((0,), unroll=True)
    row_of_sums(0)

    seam_squares = jnp.zeros((16, LANES), F32)
    for b in range(tiles):
        lanes = pl.ds(b * LANES, LANES)
        firsts = [
            toep[(b * in_tile + g) * TAPS : (b * in_tile + g) * TAPS + 16, 0:TAPS]
            for g in range(in_tile)
        ]
        added = jnp.dot(
            jnp.concatenate(firsts, axis=0), head_only[:, lanes], preferred_element_type=F32
        )
        out = seam[:, lanes] + chosen(added, 16)
        seam_squares = seam_squares + gate(TAPS, 16, lanes, out)
    squares[TAPS : TAPS + 16, :] = seam_squares

    row_of_sums(1)
    parts[mine] = part[...]

    for peer in mp_peers:
        pltpu.make_async_remote_copy(
            src_ref=part,
            dst_ref=parts.at[mine],
            send_sem=send3,
            recv_sem=recv3,
            device_id={"mp": peer},
            device_id_type=MESH,
        ).start()
    if n_mp > 1:
        peers = pl.ds(0, n_mp - 1)
        pltpu.make_async_copy(parts.at[peers], parts.at[peers], recv3).wait()
    total = jnp.sum(parts[...], axis=0)
    token = lax.broadcasted_iota(jnp.int32, (1, ROWS), 1)
    scale = lax.rsqrt(total / (WIDTH * n_mp) + EPSILON)
    scale_ref[...] = jnp.where(token < length, scale, 0.0)

    pltpu.make_async_copy(msg.at[others], msg.at[others], send1).wait()
    pltpu.make_async_copy(fwd.at[others], fwd.at[others], send2).wait()
    if n_mp > 1:
        pltpu.make_async_copy(parts.at[peers], parts.at[peers], send3).wait()


def finish(gated, resid, scale_ref, gain_ref, mixed_hbm, normed_hbm, normed, sem):
    stores = [pltpu.make_async_copy(gated, mixed_hbm, sem.at[0])]
    stores[0].start()
    gain = gain_ref[...].astype(F32).reshape(1, WIDTH)
    for blk in range(ROWS // TAPS):
        rows = pl.ds(blk * TAPS, TAPS)
        factor = jnp.broadcast_to(scale_ref[:, blk * TAPS : (blk + 1) * TAPS], (TAPS, LANES)).T
        for b in range(WIDTH // LANES):
            lanes = slice(b * LANES, (b + 1) * LANES)
            total = resid[rows, lanes].astype(F32) + gated[rows, lanes].astype(F32)
            normed[rows, lanes] = (total * factor * gain[:, lanes]).astype(BF16)
        stores.append(
            pltpu.make_async_copy(normed.at[rows], normed_hbm.at[rows], sem.at[1 + blk])
        )
        stores[-1].start()
    for store in stores:
        store.wait()


def body(n_seq, n_mp, queries, keys_in, values_in, residual, short_taps, mr_filter, norm_gain, predecessor, stretch_lengths):
    whole = pl.BlockSpec(memory_space=pltpu.HBM)
    scalars = pl.BlockSpec(memory_space=pltpu.SMEM)
    slots = (n_seq, TILE // QUAD + 1, QUAD, LANES)
    share, groups = mr_filter.shape
    out = jax.ShapeDtypeStruct((ROWS, WIDTH), BF16)
    row = pl.BlockSpec(memory_space=pltpu.VMEM)
    gated, resid, scale, gain = pl.pallas_call(
        functools.partial(kernel, n_seq, n_mp),
        out_shape=(pltpu.VMEM((ROWS, WIDTH), BF16), pltpu.VMEM((ROWS, WIDTH), BF16), pltpu.VMEM((1, ROWS), F32), pltpu.VMEM((WIDTH,), BF16)),
        in_specs=[whole] * 7 + [scalars] * 2,
        out_specs=(row, row, row, row),
        scratch_shapes=[
            pltpu.VMEM((PAD + ROWS, WIDTH), BF16),
            pltpu.VMEM((PAD + ROWS, WIDTH), BF16),
            pltpu.VMEM((PAD + ROWS, WIDTH), BF16),
            pltpu.VMEM((3, SHORT, WIDTH), BF16),
            pltpu.VMEM((share, groups), BF16),
            pltpu.VMEM((24, WIDTH), F32),
            pltpu.VMEM((ROWS, WIDTH), F32),
            pltpu.VMEM((TAPS + ROWS, WIDTH), BF16),
            *[pltpu.VMEM(slots, BF16)] * 4,
            pltpu.VMEM((LANES, LANES), F32),
            pltpu.VMEM((groups * TAPS, 2 * TAPS), BF16),
            pltpu.VMEM((groups, LANES), F32),
            pltpu.VMEM((ROWS, LANES), F32),
            pltpu.VMEM((16, WIDTH), F32),
            pltpu.VMEM((TAPS, WIDTH), BF16),
            pltpu.VMEM((1, ROWS), F32),
            pltpu.VMEM((n_mp, 1, ROWS), F32),
            pltpu.SemaphoreType.DMA((9,)),
            *[pltpu.SemaphoreType.DMA] * 6,
        ],
        compiler_params=pltpu.CompilerParams(
            collective_id=0, has_side_effects=True, vmem_limit_bytes=LIMIT
        ),
    )(
        queries,
        keys_in,
        values_in,
        residual,
        short_taps,
        mr_filter,
        norm_gain,
        predecessor,
        stretch_lengths,
    )
    return pl.pallas_call(
        finish,
        out_shape=(out, out),
        in_specs=[row, row, row, row],
        out_specs=(whole, whole),
        scratch_shapes=[
            pltpu.VMEM((ROWS, WIDTH), BF16),
            pltpu.SemaphoreType.DMA((1 + ROWS // TAPS,)),
        ],
        compiler_params=pltpu.CompilerParams(vmem_limit_bytes=16 * 1024 * 1024),
    )(gated, resid, scale, gain)


def solution(mesh):
    in_specs = (
        P("seq", "mp"),
        P("seq", "mp"),
        P("seq", "mp"),
        P("seq", "mp"),
        P(None, None, "mp"),
        P("seq", "mp"),
        P("mp"),
        P(),
        P(),
    )
    out_specs = (P("seq", "mp"), P("seq", "mp"))
    return jax.shard_map(
        functools.partial(body, mesh.shape["seq"], mesh.shape["mp"]),
        mesh=mesh,
        in_specs=in_specs,
        out_specs=out_specs,
        check_vma=False,
    )
```
